256 devices in a mesh: pos: 32 (over z_lo, x, core), chan: 8 (over z_hi, y).
Axes of the slice: x: 4, y: 4, z: 8 (z_hi: 2, z_lo: 4; z = z_hi * 4 + z_lo), core: 2. Of those that a mesh axis runs over, the one named last changes fastest.
Arguments:
- prompt_signal: bfloat16 [8192, 8192], P('pos', 'chan'), may hold values from -6 to 6
- long_filter: bfloat16 [2, 8192, 8192], P(None, 'pos', 'chan'), may hold values from -1 to 1, as said below
- sample_tokens: int32 [1024, 4], P('pos'), may hold values from 0 to 255
- token_features: bfloat16 [256, 3, 8192], P(None, None, 'chan'), may hold values from -6 to 6
- out_weight: bfloat16 [8192, 4096], P('chan'), may hold values from -0.0625 to 0.0625
Outputs:
- contributions: bfloat16 [8192, 8192], P('pos', 'chan')
- decoded: bfloat16 [1024, 4, 4096], P('pos', None, 'chan')
The draws below stay inside these ranges and needn't reach their ends.
Inputs may be any that keep to these rules, and one draw needn't show every extreme that they name: `long_filter`: each entry of the filter lies between the bounds.
All inputs are finite; a program needn't handle non-finite values.
Results may differ from the reference program's by a relative error of at most 0.015.
Values may be sent and summed in bfloat16 or wider, within the bound.
A program may use at most 128 MiB of HBM per device.

```python
import math
import jax
import jax.numpy as jnp
from jax import lax

D = 8192
VOCAB = 256
DOUT = 4096
STEPS = 4
PROMPT = 8192
SAMPLES = 1024


def draw_long_filter(key, part):
    key = jax.random.fold_in(key, 7)
    noise_key, rate_key = jax.random.split(key)
    noise = jnp.clip(jax.random.normal(noise_key, (2, PROMPT, D), jnp.float32), -4.0, 4.0)
    lowest = jnp.log(30.0)
    highest = jnp.log(2.0 * PROMPT)
    spans = jnp.exp(jax.random.uniform(rate_key, (D,), jnp.float32, lowest, highest))
    lag_values = (jnp.arange(2)[:, None] * PROMPT + jnp.arange(PROMPT)[None, :]).astype(jnp.float32)
    envelope = jnp.exp(-lag_values[:, :, None] / spans[None, None, :])
    scaled = jnp.sqrt(2.0 / spans)[None, None, :] * envelope * noise * 0.95
    return scaled.astype(jnp.bfloat16)


def with_ends(values, stream_key, least, high):
    longest = values.shape.index(max(values.shape))
    spots = []
    for shift in (0, 1):
        where = [jax.random.randint(jax.random.fold_in(stream_key, axis), (), 0, length) for axis, length in enumerate(values.shape)]
        where[longest] = (where[longest] + shift) % values.shape[longest]
        spots.append(tuple(where))
    return values.at[spots[0]].set(least).at[spots[1]].set(high)


def levels(rng, extent, shards, smallest, largest):
    loudness = 1.0
    for position, parts in shards:
        heights = jax.random.uniform(jax.random.fold_in(jax.random.fold_in(rng, 6), position), (parts,), jnp.float32, smallest / len(shards), largest / len(shards))
        loudness = loudness * jnp.repeat(jnp.exp(heights), extent[position] // parts).reshape((-1,) + (1,) * (len(extent) - 1 - position))
    return loudness


def gaussian(rng, dims, spread, bound, shards=(), dtype=jnp.bfloat16):
    entries = jax.random.normal(rng, dims, jnp.float32) * spread
    if len(shards) > 0:
        entries = levels(rng, dims, shards, -0.22, 0.18) * entries
    return jnp.clip(entries, min=-bound, max=bound).astype(dtype)


def setup_inputs(seed: int = 0) -> dict:
    streams_of = jax.random.split(jax.random.key(seed), 6)
    return {
        "prompt_signal": gaussian(streams_of[0], (PROMPT, D), 1.0, 6.0, ((0, 32), (1, 8))),
        "long_filter": draw_long_filter(jax.random.fold_in(streams_of[5], 71), 0),
        "sample_tokens": with_ends(jax.random.randint(streams_of[2], (SAMPLES, STEPS), 0, VOCAB), jax.random.fold_in(streams_of[2], 1), 0, VOCAB - 1).astype(jnp.int32),
        "token_features": gaussian(streams_of[3], (VOCAB, 3, D), 1.0, 6.0, ((2, 8),)),
        "out_weight": gaussian(streams_of[4], (D, DOUT), D ** -0.5, 0.0625, ((0, 8),)),
    }


def reference(prompt_signal, long_filter, sample_tokens, token_features, out_weight):
    lags = long_filter.reshape(2 * PROMPT, D)
    width = math.gcd(D, 512)
    starts = (jnp.arange(D // width) * width).astype(jnp.int32)

    def block_conv(start):
        signal = lax.dynamic_slice_in_dim(prompt_signal, start, width, 1).astype(jnp.float32)
        kernel = lax.dynamic_slice_in_dim(lags, start, width, 1).astype(jnp.float32)
        spectrum = jnp.fft.rfft(signal, n=2 * PROMPT, axis=0) * jnp.fft.rfft(kernel, axis=0)
        return jnp.fft.irfft(spectrum, n=2 * PROMPT, axis=0)[PROMPT:]

    blocks = lax.map(block_conv, starts)
    contributions = jnp.transpose(blocks, (1, 0, 2)).reshape(PROMPT, D).astype(jnp.bfloat16)

    looked = token_features[sample_tokens].astype(jnp.float32)
    query = looked[:, :, 0]
    own = looked[:, :, 1] * looked[:, :, 2]
    filt_head = long_filter[0, :STEPS].astype(jnp.float32)
    seeds = contributions[:STEPS].astype(jnp.float32)
    columns = []
    for current in range(STEPS):
        mixed = jnp.broadcast_to(seeds[current], own[:, current].shape)
        for earlier in range(current + 1):
            mixed = mixed + filt_head[current - earlier] * own[:, earlier]
        columns.append(mixed)
    mixed_all = jnp.stack(columns, 1)
    gated = (query * mixed_all).astype(jnp.bfloat16)
    decoded = jnp.dot(gated.reshape(-1, D), out_weight, preferred_element_type=jnp.float32)
    decoded = decoded.reshape(SAMPLES, STEPS, DOUT).astype(jnp.bfloat16)
    return contributions, decoded
```

```python
import functools
import math

import jax
import jax.numpy as jnp
import numpy as np
from jax import lax
from jax.experimental import pallas as pl
from jax.experimental.pallas import tpu as pltpu
from jax.sharding import PartitionSpec as P

MESH = pl.DeviceIdType.MESH
LANES = 128
GROUP = 16
F32 = jnp.float32
BF16 = jnp.bfloat16
NT = (((1,), (1,)), ((), ()))


def turn(value, cosine, sine):
    re, im = value
    near = lambda a, b: abs(a - b) < 1e-12
    if near(sine, 0.0):
        return (re, im) if cosine > 0 else (-re, -im)
    if near(cosine, 0.0):
        return (-im, re) if sine > 0 else (im, -re)
    if near(abs(cosine), abs(sine)):
        scale = abs(cosine)
        a, b = math.copysign(1, cosine), math.copysign(1, sine)
        if a > 0:
            return ((re - im if b > 0 else re + im) * scale, (im + re if b > 0 else im - re) * scale)
        return ((re + im if b > 0 else re - im) * -scale, (im - re if b > 0 else im + re) * -scale)
    return (re * cosine - im * sine, re * sine + im * cosine)


def spin(value, index, period, sign):
    angle = 2.0 * math.pi * index / period
    return turn(value, math.cos(angle), sign * math.sin(angle))


def fft(values, sign):
    size = len(values)
    if size == 1:
        return values
    even, odd = fft(values[::2], sign), fft(values[1::2], sign)
    low, high = [], []
    for k in range(size // 2):
        (er, ei), (tr, ti) = even[k], spin(odd[k], k, size, sign)
        low.append((er + tr, ei + ti))
        high.append((er - tr, ei - ti))
    return low + high


def frequency_order(blocks):
    order = [4 * q + 1 for q in range(blocks // 2)]
    size, factor = blocks, 2
    while size >= 4:
        order += [factor * (4 * q + 1) for q in range(size // 4)]
        size, factor = size // 2, factor * 2
    return order + [0, blocks]


def outer_forward(blocks, same, diff, put):
    half = blocks // 2
    held = [spin((diff(n), -diff(n + half)), n, 2 * blocks, -1) for n in range(half)]
    slot = 0
    for re, im in fft(held, -1):
        put(slot, re, im)
        slot += 1
    size = blocks
    real = [(same(n), same(n + half)) for n in range(half)]
    while size >= 4:
        half, quarter = size // 2, size // 4
        lower = [a + b for a, b in real]
        away = [a - b for a, b in real]
        held = [spin((away[n], -away[n + quarter]), n, size, -1) for n in range(quarter)]
        for re, im in fft(held, -1):
            put(slot, re, im)
            slot += 1
        real = [(lower[n], lower[n + quarter]) for n in range(quarter)]
        size = half
    first, second = real[0]
    put(slot, first + second, None)
    put(slot + 1, first - second, None)


def outer_backward(blocks, take, put):
    first, last = take(blocks - 1)[0] * 0.5, take(blocks)[0] * 0.5
    real = [first + last, first - last]
    size, start = 4, blocks - 2
    while size <= blocks:
        quarter = size // 4
        back = fft([take(start + q) for q in range(quarter)], 1)
        back = [spin(value, n, size, 1) for n, value in enumerate(back)]
        wave = [re for re, _ in back] + [-im for _, im in back]
        real = [a + b for a, b in zip(real, wave)] + [a - b for a, b in zip(real, wave)]
        size, start = size * 2, start - size // 2
    half = blocks // 2
    back = fft([take(q) for q in range(half)], 1)
    for n, value in enumerate(back):
        re, im = spin(value, n, 2 * blocks, 1)
        put(n, real[n] - re)
        put(n + half, real[n + half] + im)


def tables(blocks, rows):
    order = np.array(frequency_order(blocks))
    length = 2 * blocks * rows
    inner = np.arange(rows)
    angle = 2.0 * np.pi * (order[:, None] * inner[None, :] % length) / length
    twiddle = np.stack([np.cos(angle), -np.sin(angle)], 1).astype(np.float32)
    twiddle = np.repeat(twiddle[:, :, None, :], 8, 2)
    angle = 2.0 * np.pi * (inner[:, None] * inner[None, :] % rows) / rows
    cosine, sine = np.cos(angle), np.sin(angle)
    forward = np.block([[cosine, -sine], [sine, cosine]]).astype(np.float32)
    backward = (forward.T / (blocks * rows)).astype(np.float32)

    def split(table):
        high = table.astype(jnp.bfloat16)
        return [high, (table - high.astype(np.float32)).astype(jnp.bfloat16)]

    return twiddle, np.stack(split(forward) + split(backward))


def kernel(
    blocks, chans, zs, signal, filt, tokens, features, weight, twiddle_in, dft_in,
    contrib, decoded,
    send_x, send_f, send_g, recv_x, recv_f, recv_g, send_o, recv_o,
    work, wave, spec_x, spec_h, shifted,
    corr_send, corr_recv, seed_send, seed_recv, rows_held,
    feats, weights, twiddle, dft, query, own, gated,
    part_send, part_recv, part_own, last_send, last_recv,
    local_sem, send_sem, recv_sem,
):
    me, chan = lax.axis_index("pos"), lax.axis_index("chan")
    rows, width = signal.shape
    mine = width // blocks
    slots = blocks + 1
    chunks = mine // GROUP
    per = LANES // mine
    strips = width // LANES
    ys = chans // zs
    z_here, y_here = chan // ys, lax.rem(chan, ys)
    steps = tokens.shape[0]
    samples = tokens.shape[1]
    columns = decoded.shape[2]

    loads = [
        pltpu.make_async_copy(src, dst, local_sem.at[i])
        for i, (src, dst) in enumerate(
            ((dft_in, dft), (twiddle_in, twiddle), (features, feats), (weight, weights))
        )
    ]
    for load in loads:
        load.start()

    barrier = pltpu.get_barrier_semaphore()

    def greet(i, carry):
        pl.semaphore_signal(
            barrier, inc=1, device_id={"pos": lax.rem(me + i, blocks)}, device_id_type=MESH
        )
        return carry

    lax.fori_loop(1, blocks, greet, 0)
    for i in range(1, ys):
        there = z_here * ys + lax.rem(y_here + i, ys)
        pl.semaphore_signal(barrier, inc=1, device_id={"chan": there}, device_id_type=MESH)
    for i in range(1, zs):
        there = lax.rem(z_here + i, zs) * ys + y_here
        pl.semaphore_signal(barrier, inc=1, device_id={"chan": there}, device_id_type=MESH)

    def eye(size):
        return (
            lax.broadcasted_iota(jnp.int32, (size, size), 0)
            == lax.broadcasted_iota(jnp.int32, (size, size), 1)
        ).astype(F32).astype(BF16)

    eye_lanes, eye_rows = eye(LANES), eye(rows)

    def flipped(block):
        turned = lax.dot_general(eye_lanes, block, NT, preferred_element_type=F32)
        return turned.astype(BF16)

    for s in range(strips):
        strip = pl.ds(s * LANES, LANES)
        owners = pl.ds(s * per, per)
        send_x[owners] = flipped(signal[:, strip]).reshape(per, mine, rows)
    pl.semaphore_wait(barrier, (blocks - 1) + (ys - 1) + (zs - 1))

    def spread(source, target, slot):
        def one(i, carry):
            there = lax.rem(me + i, blocks)
            pltpu.make_async_remote_copy(
                src_ref=source(there),
                dst_ref=target,
                send_sem=send_sem.at[slot],
                recv_sem=recv_sem.at[slot],
                device_id={"pos": there},
                device_id_type=MESH,
            ).start()
            return carry

        lax.fori_loop(1, blocks, one, 0)

    def all_of(source, target, slot):
        others = pl.ds(0, blocks - 1)
        return pltpu.make_async_remote_copy(
            src_ref=source.at[others],
            dst_ref=target.at[others],
            send_sem=send_sem.at[slot],
            recv_sem=recv_sem.at[slot],
            device_id={"pos": lax.rem(me + 1, blocks)},
            device_id_type=MESH,
        )

    spread(lambda there: send_x.at[there], recv_x.at[me], 0)
    recv_x[me] = send_x[me]
    for s in range(strips):
        strip = pl.ds(s * LANES, LANES)
        send_f[pl.ds(s * per, per)] = flipped(filt[0, :, strip]).reshape(per, mine, rows)
    spread(lambda there: send_f.at[there], recv_f.at[me], 1)
    recv_f[me] = send_f[me]

    lane = lax.broadcasted_iota(jnp.int32, (1, LANES), 1)

    @pl.when(me == 0)
    def _():
        x_head = signal[0:16, :].astype(F32)
        g_head = filt[1, 0:16, :].astype(F32)
        for t in range(steps):
            row = x_head[0:1] * g_head[t : t + 1]
            for r in range(1, t + 1):
                row = row + x_head[r : r + 1] * g_head[t - r : t - r + 1]
            for s in range(strips):
                part = row[:, s * LANES : (s + 1) * LANES]
                for i in range(per):
                    shift = (t * mine - i * mine) % LANES
                    moved = pltpu.roll(part, shift, 1) if shift else part
                    inside = (lane >= t * mine) & (lane < (t + 1) * mine)
                    before = corr_send[s * per + i] if t else jnp.zeros((1, LANES), F32)
                    corr_send[s * per + i] = jnp.where(inside, moved, before)
        spread(lambda there: corr_send.at[there], corr_recv, 2)
        corr_recv[...] = corr_send[0]

    for s in range(strips):
        strip = pl.ds(s * LANES, LANES)
        turned = flipped(filt[1, :, strip]).reshape(per, chunks, GROUP, rows)
        for k in range(chunks):
            send_g[k, pl.ds(s * per, per)] = turned[:, k]
    for k in range(chunks):
        recv_g[k, me] = send_g[k, me]
    spread(lambda there: send_g.at[0, there], recv_g.at[0, me], 3)

    loads[0].wait()
    loads[1].wait()
    loads[2].wait()

    vocab = feats.shape[1]
    for t in range(steps):
        row = tokens[t : t + 1, :].astype(F32)
        where_ = lax.broadcasted_iota(jnp.int32, (samples, samples), 0) == lax.broadcasted_iota(
            jnp.int32, (samples, samples), 1
        )
        column = jnp.sum(jnp.where(where_, row, 0.0), axis=1, keepdims=True).astype(jnp.int32)
        hot = (column == lax.broadcasted_iota(jnp.int32, (samples, vocab), 1)).astype(F32).astype(BF16)
        part = pl.ds(t * samples, samples)
        query[part] = jnp.dot(hot, feats[0], preferred_element_type=F32).astype(BF16)
        own[part] = jnp.dot(hot, feats[1], preferred_element_type=F32) * jnp.dot(
            hot, feats[2], preferred_element_type=F32
        )

    def tiles(body):
        halves = rows // LANES

        def step(i, carry):
            top = pl.multiple_of((i // halves) * 8, 8)
            left = pl.multiple_of(lax.rem(i, halves) * LANES, LANES)
            body(pl.ds(top, 8), left)
            return carry

        lax.fori_loop(0, (GROUP // 8) * halves, step, 0)

    def forward_tile(same, diff):
        def body(top, left):
            across = pl.ds(left, LANES)
            imag = pl.ds(pl.multiple_of(left + rows, LANES), LANES)

            def put(slot, re, im):
                c, s = twiddle[slot, 0, :, across], twiddle[slot, 1, :, across]
                if im is None:
                    wave[slot, top, across] = re * c
                    wave[slot, top, imag] = re * s
                else:
                    wave[slot, top, across] = re * c - im * s
                    wave[slot, top, imag] = re * s + im * c

            outer_forward(
                blocks,
                lambda n: work[same, n, top, across],
                lambda n: work[diff, n, top, across],
                put,
            )

        return body

    def backward_tile(top, left):
        across = pl.ds(left, LANES)
        imag = pl.ds(pl.multiple_of(left + rows, LANES), LANES)

        def take(slot):
            c, s = twiddle[slot, 0, :, across], twiddle[slot, 1, :, across]
            re, im = wave[slot, top, across], wave[slot, top, imag]
            return re * c + im * s, im * c - re * s

        def put(n, value):
            work[0, n, top, across] = value

        outer_backward(blocks, take, put)

    group = max(g for g in range(1, 12) if slots % g == 0)

    def split(value):
        high = value.astype(BF16)
        return high, (value - high.astype(F32)).astype(BF16)

    def inner(value, table):
        high, low = split(value)
        dot = functools.partial(jnp.dot, preferred_element_type=F32)
        return dot(high, dft[table]) + dot(low, dft[table]) + dot(high, dft[table + 1])

    def by_slots(body):
        def step(i, carry):
            body(pl.ds(i * group, group))
            return carry

        lax.fori_loop(0, slots // group, step, 0)

    flat = (group * GROUP, 2 * rows)
    deep = (group, GROUP, 2 * rows)

    all_of(send_x, recv_x, 0).wait_recv()
    for k in range(chunks):
        part = pl.ds(k * GROUP, GROUP)

        def widen(n, carry):
            work[0, n] = recv_x[n, part, :].astype(F32)
            return carry

        lax.fori_loop(0, blocks, widen, 0)
        tiles(forward_tile(0, 0))

        def to_spectrum(which, k=k):
            spec_x[k, which] = inner(wave[which].reshape(flat), 0).reshape(deep)

        by_slots(to_spectrum)

    row_id = lax.broadcasted_iota(jnp.int32, (rows, rows), 0)
    col_id = lax.broadcasted_iota(jnp.int32, (rows, rows), 1)
    bundle = 8 if blocks % 8 == 0 else blocks
    for t in range(steps):
        back = ((row_id + col_id == t) | (row_id + col_id == t + rows)).astype(F32).astype(BF16)

        def reverse(i, carry, t=t, back=back):
            which = pl.ds(i * bundle, bundle)
            taken = recv_x[which].reshape(bundle * mine, rows)
            turned = jnp.dot(taken, back, preferred_element_type=F32).astype(BF16)
            shifted[t, which] = turned.reshape(bundle, mine, rows)
            return carry

        lax.fori_loop(0, blocks // bundle, reverse, 0)

    all_of(send_f, recv_f, 1).wait_recv()
    lanes_here = lax.broadcasted_iota(jnp.int32, (mine, LANES), 1)

    def add_block(n, sums, first):
        near = recv_f[blocks - 1 - n].astype(F32)
        if not first:
            far = recv_f[blocks - n, :, 0:LANES].astype(F32)
        result = []
        for t in range(steps):
            x = shifted[t, n].astype(F32)
            other = jnp.zeros((mine, LANES), F32) if first else far
            total = x[:, 0:LANES] * jnp.where(lanes_here > t, near[:, 0:LANES], other)
            for h in range(1, rows // LANES):
                total = total + x[:, h * LANES : (h + 1) * LANES] * near[:, h * LANES : (h + 1) * LANES]
            result.append(sums[t] + total)
        return tuple(result)

    sums = add_block(0, tuple(jnp.zeros((mine, LANES), F32) for _ in range(steps)), True)
    sums = lax.fori_loop(1, blocks, lambda n, c: add_block(n, c, False), sums)
    channel = lax.broadcasted_iota(jnp.int32, (mine, LANES), 0)
    head = recv_f[0, :, 0:LANES].astype(F32)
    seed_rows = jnp.zeros((mine, LANES), F32)
    head_rows = jnp.zeros((mine, LANES), F32)
    for t in range(steps):
        place = lanes_here == t * mine + channel
        seed_rows += jnp.where(place, jnp.sum(sums[t], axis=1, keepdims=True), 0.0)
        value = jnp.sum(jnp.where(lanes_here == t, head, 0.0), axis=1, keepdims=True)
        head_rows += jnp.where(place, value, 0.0)

    @pl.when(me != 0)
    def _():
        pltpu.make_async_remote_copy(
            src_ref=corr_send.at[0], dst_ref=corr_recv, send_sem=send_sem.at[2],
            recv_sem=recv_sem.at[2], device_id={"pos": 0}, device_id_type=MESH,
        ).wait_recv()

    seed_row = jnp.sum(seed_rows, axis=0, keepdims=True) + corr_recv[...]
    seed_send[:, 0:LANES] = seed_row.astype(BF16).astype(F32)
    seed_send[:, LANES : 2 * LANES] = jnp.sum(head_rows, axis=0, keepdims=True)
    spread(lambda there: seed_send, seed_recv.at[me], 4)
    seed_recv[me] = seed_send[...]
    for k in range(1, chunks):
        spread(lambda there, k=k: send_g.at[k, there], recv_g.at[k, me], 3 + 2 * k)

    def convolve(k):
        slot = 3 + 2 * k
        all_of(send_g.at[k], recv_g.at[k], slot).wait_recv()
        part = pl.ds(k * GROUP, GROUP)

        def widen(n, carry):
            early, late = recv_f[n, part, :].astype(F32), recv_g[k, n].astype(F32)
            work[0, n] = early + late
            work[1, n] = early - late
            return carry

        lax.fori_loop(0, blocks, widen, 0)
        tiles(forward_tile(0, 1))

        def through(which):
            h = inner(wave[which].reshape(flat), 0)
            x = spec_x[k, which].reshape(flat)
            hr, hi, xr, xi = h[:, :rows], h[:, rows:], x[:, :rows], x[:, rows:]
            spec_h[:, 0:rows] = hr * xr - hi * xi
            spec_h[:, rows : 2 * rows] = hr * xi + hi * xr
            wave[which] = inner(spec_h[...], 2).reshape(deep)

        by_slots(through)
        tiles(backward_tile)

        def narrow(n, carry):
            send_o[n, k] = work[0, n].astype(BF16)
            return carry

        lax.fori_loop(0, blocks, narrow, 0)
        spread(lambda there: send_o.at[there, k], recv_o.at[me, k], 6 + 2 * k)
        recv_o[me, k] = send_o[me, k]

    def decode():
        all_of(seed_recv, seed_recv, 4).wait_recv()
        which = lax.broadcasted_iota(jnp.int32, (blocks, LANES), 1) // mine
        mod = lax.rem(lax.broadcasted_iota(jnp.int32, (blocks, LANES), 0), per)
        pick = (
            lax.broadcasted_iota(jnp.int32, (strips, blocks), 1) // per
            == lax.broadcasted_iota(jnp.int32, (strips, blocks), 0)
        ).astype(F32).astype(BF16)
        for part in range(2):
            taken = seed_recv[:, 0, part * LANES : (part + 1) * LANES]
            for t in range(steps):
                lined = jnp.zeros((blocks, LANES), F32)
                for i in range(per):
                    shift = ((i - t) * mine) % LANES
                    moved = pltpu.roll(taken, shift, 1) if shift else taken
                    lined = jnp.where((which == i) & (mod == i), moved, lined)
                rows_held[part * steps + t] = jnp.dot(
                    pick, lined.astype(BF16), preferred_element_type=F32
                )
        loads[3].wait()

        for s in range(strips):
            strip = pl.ds(s * LANES, LANES)
            for t in range(steps):
                total = jnp.broadcast_to(rows_held[t, s : s + 1, :], (samples, LANES))
                for r in range(t + 1):
                    lag = rows_held[steps + t - r, s : s + 1, :]
                    total = total + lag * own[pl.ds(r * samples, samples), strip]
                part = pl.ds(t * samples, samples)
                gated[part, strip] = (query[part, strip].astype(F32) * total).astype(BF16)

        def product(z, y):
            start = pl.multiple_of((z * ys + y) * columns, LANES)
            return jnp.dot(
                gated[...], weights[:, pl.ds(start, columns)], preferred_element_type=F32
            )

        def to_y(i, carry):
            there = lax.rem(y_here + i, ys)
            for z in range(zs):
                part_send[there, z] = product(z, there).astype(BF16)
            pltpu.make_async_remote_copy(
                src_ref=part_send.at[there], dst_ref=part_recv.at[y_here], send_sem=send_sem.at[7],
                recv_sem=recv_sem.at[7], device_id={"chan": z_here * ys + there}, device_id_type=MESH,
            ).start()
            return carry

        if ys > 1:
            lax.fori_loop(1, ys, to_y, 0)
        for z in range(zs):
            part_own[z] = product(z, y_here)

    y_all = None
    if ys > 1:
        others = pl.ds(0, ys - 1)
        y_all = pltpu.make_async_remote_copy(
            src_ref=part_send.at[others], dst_ref=part_recv.at[others], send_sem=send_sem.at[7],
            recv_sem=recv_sem.at[7], device_id={"chan": z_here * ys + lax.rem(y_here + 1, ys)},
            device_id_type=MESH,
        )
    z_copy = pltpu.make_async_remote_copy(
        src_ref=last_send, dst_ref=last_recv, send_sem=send_sem.at[9], recv_sem=recv_sem.at[9],
        device_id={"chan": lax.rem(z_here + 1, zs) * ys + y_here}, device_id_type=MESH,
    )

    def add_y():
        def one(i, carry):
            there = lax.rem(y_here + i, ys)
            for z in range(zs):
                part_own[z] += part_recv[there, z].astype(F32)
            return carry

        if ys > 1:
            y_all.wait_recv()
            lax.fori_loop(1, ys, one, 0)
        last_send[...] = part_own[1 - z_here].astype(BF16)
        z_copy.start()

    decode()
    for k in range(chunks):
        convolve(k)
        if k == 0:
            add_y()

    z_copy.wait_recv()
    result = (part_own[z_here] + last_recv[...].astype(F32)).astype(BF16)
    decoded[...] = result.reshape(steps, samples, columns)

    for k in range(chunks):
        all_of(send_o.at[:, k], recv_o.at[:, k], 6 + 2 * k).wait_recv()
    for s in range(strips):
        taken = recv_o[pl.ds(s * per, per)].reshape(LANES, rows)
        turned = lax.dot_general(eye_rows, taken, NT, preferred_element_type=F32)
        contrib[:, pl.ds(s * LANES, LANES)] = turned.astype(BF16)

    all_of(send_x, recv_x, 0).wait_send()
    all_of(send_f, recv_f, 1).wait_send()

    @pl.when(me == 0)
    def _():
        all_of(corr_send, corr_send, 2).wait_send()

    for k in range(chunks):
        all_of(send_g.at[k], recv_g.at[k], 3 + 2 * k).wait_send()
        all_of(send_o.at[:, k], recv_o.at[:, k], 6 + 2 * k).wait_send()
    all_of(seed_recv, seed_recv, 4).wait_send()
    if ys > 1:
        y_all.wait_send()
    z_copy.wait_send()


def per_device(chans, prompt_signal, long_filter, sample_tokens, token_features, out_weight):
    blocks = lax.axis_size("pos")
    rows, width = prompt_signal.shape
    samples, steps = sample_tokens.shape
    mine = width // blocks
    slots = blocks + 1
    chunks = mine // GROUP
    zs = 2
    ys = chans // zs
    columns = out_weight.shape[1] // chans
    twiddle, dft = tables(blocks, rows)
    group = max(g for g in range(1, 12) if slots % g == 0)
    vmem, dma = pltpu.VMEM, pltpu.SemaphoreType.DMA
    by_vmem = pl.BlockSpec(memory_space=pltpu.VMEM)
    by_hbm = pl.BlockSpec(memory_space=pl.ANY)
    count = steps * samples
    contributions, decoded = pl.pallas_call(
        functools.partial(kernel, blocks, chans, zs),
        out_shape=(
            jax.ShapeDtypeStruct((rows, width), BF16),
            jax.ShapeDtypeStruct((steps, samples, columns), BF16),
        ),
        in_specs=[by_vmem, by_vmem, by_vmem, by_hbm, by_hbm, by_hbm, by_hbm],
        out_specs=(by_vmem, by_vmem),
        scratch_shapes=[
            vmem((blocks, mine, rows), BF16),
            vmem((blocks, mine, rows), BF16),
            vmem((chunks, blocks, GROUP, rows), BF16),
            vmem((blocks, mine, rows), BF16),
            vmem((blocks, mine, rows), BF16),
            vmem((chunks, blocks, GROUP, rows), BF16),
            vmem((blocks, chunks, GROUP, rows), BF16),
            vmem((blocks, chunks, GROUP, rows), BF16),
            vmem((2, blocks, GROUP, rows), F32),
            vmem((slots, GROUP, 2 * rows), F32),
            vmem((chunks, slots, GROUP, 2 * rows), F32),
            vmem((group * GROUP, 2 * rows), F32),
            vmem((steps, blocks, mine, rows), BF16),
            vmem((blocks, 1, LANES), F32),
            vmem((1, LANES), F32),
            vmem((1, 2 * LANES), F32),
            vmem((blocks, 1, 2 * LANES), F32),
            vmem((2 * steps, width // LANES, LANES), F32),
            vmem((3, token_features.shape[0], width), BF16),
            vmem(out_weight.shape, BF16),
            vmem(twiddle.shape, F32),
            vmem(dft.shape, BF16),
            vmem((count, width), BF16),
            vmem((count, width), F32),
            vmem((count, width), BF16),
            vmem((ys, zs, count, columns), BF16),
            vmem((ys, zs, count, columns), BF16),
            vmem((zs, count, columns), F32),
            vmem((count, columns), BF16),
            vmem((count, columns), BF16),
            dma((4,)),
            dma((10,)),
            dma((10,)),
        ],
        compiler_params=pltpu.CompilerParams(
            collective_id=0, has_side_effects=True, vmem_limit_bytes=50 * 2**20
        ),
        name="conv_decode",
    )(
        prompt_signal,
        long_filter,
        sample_tokens.T,
        jnp.transpose(token_features, (1, 0, 2)),
        out_weight,
        jnp.asarray(twiddle),
        jnp.asarray(dft),
    )
    return contributions, jnp.transpose(decoded, (1, 0, 2))


def solution(mesh):
    placed = (
        P("pos", "chan"),
        P(None, "pos", "chan"),
        P("pos", None),
        P(None, None, "chan"),
        P("chan", None),
    )
    return jax.shard_map(
        functools.partial(per_device, mesh.shape["chan"]),
        mesh=mesh,
        in_specs=placed,
        out_specs=(P("pos", "chan"), P("pos", None, "chan")),
        check_vma=False,
    )
```

```python
import functools
import math

import jax
import jax.numpy as jnp
import numpy as np
from jax import lax
from jax.experimental import pallas as pl
from jax.experimental.pallas import tpu as pltpu
from jax.sharding import PartitionSpec as P

MESH = pl.DeviceIdType.MESH
LANES = 128
GROUP = 16
F32 = jnp.float32
BF16 = jnp.bfloat16
NT = (((1,), (1,)), ((), ()))


def turn(value, cosine, sine):
    re, im = value
    near = lambda a, b: abs(a - b) < 1e-12
    if near(sine, 0.0):
        return (re, im) if cosine > 0 else (-re, -im)
    if near(cosine, 0.0):
        return (-im, re) if sine > 0 else (im, -re)
    if near(abs(cosine), abs(sine)):
        scale = abs(cosine)
        a, b = math.copysign(1, cosine), math.copysign(1, sine)
        if a > 0:
            return ((re - im if b > 0 else re + im) * scale, (im + re if b > 0 else im - re) * scale)
        return ((re + im if b > 0 else re - im) * -scale, (im - re if b > 0 else im + re) * -scale)
    return (re * cosine - im * sine, re * sine + im * cosine)


def spin(value, index, period, sign):
    angle = 2.0 * math.pi * index / period
    return turn(value, math.cos(angle), sign * math.sin(angle))


def fft(values, sign):
    size = len(values)
    if size == 1:
        return values
    even, odd = fft(values[::2], sign), fft(values[1::2], sign)
    low, high = [], []
    for k in range(size // 2):
        (er, ei), (tr, ti) = even[k], spin(odd[k], k, size, sign)
        low.append((er + tr, ei + ti))
        high.append((er - tr, ei - ti))
    return low + high


def frequency_order(blocks):
    order = [4 * q + 1 for q in range(blocks // 2)]
    size, factor = blocks, 2
    while size >= 4:
        order += [factor * (4 * q + 1) for q in range(size // 4)]
        size, factor = size // 2, factor * 2
    return order + [0, blocks]


def outer_forward(blocks, same, diff, put):
    half = blocks // 2
    held = [spin((diff(n), -diff(n + half)), n, 2 * blocks, -1) for n in range(half)]
    slot = 0
    for re, im in fft(held, -1):
        put(slot, re, im)
        slot += 1
    size = blocks
    real = [(same(n), same(n + half)) for n in range(half)]
    while size >= 4:
        half, quarter = size // 2, size // 4
        lower = [a + b for a, b in real]
        away = [a - b for a, b in real]
        held = [spin((away[n], -away[n + quarter]), n, size, -1) for n in range(quarter)]
        for re, im in fft(held, -1):
            put(slot, re, im)
            slot += 1
        real = [(lower[n], lower[n + quarter]) for n in range(quarter)]
        size = half
    first, second = real[0]
    put(slot, first + second, None)
    put(slot + 1, first - second, None)


def outer_backward(blocks, take, put):
    first, last = take(blocks - 1)[0] * 0.5, take(blocks)[0] * 0.5
    real = [first + last, first - last]
    size, start = 4, blocks - 2
    while size <= blocks:
        quarter = size // 4
        back = fft([take(start + q) for q in range(quarter)], 1)
        back = [spin(value, n, size, 1) for n, value in enumerate(back)]
        wave = [re for re, _ in back] + [-im for _, im in back]
        real = [a + b for a, b in zip(real, wave)] + [a - b for a, b in zip(real, wave)]
        size, start = size * 2, start - size // 2
    half = blocks // 2
    back = fft([take(q) for q in range(half)], 1)
    for n, value in enumerate(back):
        re, im = spin(value, n, 2 * blocks, 1)
        put(n, real[n] - re)
        put(n + half, real[n + half] + im)


def tables(blocks, rows):
    order = np.array(frequency_order(blocks))
    length, half = 2 * blocks * rows, rows // 2
    inner = np.arange(half)
    angle = 2.0 * np.pi * (order[:, None] * inner[None, :] % length) / length
    odd = angle + 2.0 * np.pi * inner[None, :] / rows
    twiddle = np.stack([np.cos(angle), -np.sin(angle), np.cos(odd), -np.sin(odd)], 1)
    twiddle = np.repeat(twiddle.astype(np.float32)[:, :, None, :], 8, 2)
    angle = 2.0 * np.pi * (inner[:, None] * inner[None, :] % half) / half
    cosine, sine = np.cos(angle), np.sin(angle)
    forward = np.block([[cosine, -sine], [sine, cosine]]).astype(np.float32)
    backward = (forward.T / (blocks * rows)).astype(np.float32)

    def split(table):
        high = table.astype(jnp.bfloat16)
        return [high, (table - high.astype(np.float32)).astype(jnp.bfloat16)]

    return twiddle, np.stack(split(forward) + split(backward))


def kernel(
    blocks, chans, zs, signal_in, filt_in, tokens_in, features, weight, twiddle_in, dft_in,
    contrib, decoded,
    signal, filt, tokens,
    send_x, send_f, send_g, recv_x, recv_f, recv_g, send_o, recv_o,
    work, wave, spec_x, spec_h, shifted,
    corr_send, corr_recv, seed_send, seed_recv, rows_held,
    feats, weights, twiddle, dft, query, own, gated,
    part_send, part_recv, part_own, last_send, last_recv,
    local_sem, send_sem, recv_sem,
):
    me, chan = lax.axis_index("pos"), lax.axis_index("chan")
    rows, width = signal.shape
    mine = width // blocks
    slots = blocks + 1
    chunks = mine // GROUP
    per = LANES // mine
    strips = width // LANES
    ys = chans // zs
    z_here, y_here = chan // ys, lax.rem(chan, ys)
    planes = blocks // 4
    mirror = (3 - me // planes) * planes + lax.rem(me, planes)
    steps = tokens.shape[1]
    samples = tokens.shape[2]
    columns = decoded.shape[2]

    loads = [
        pltpu.make_async_copy(src, dst, local_sem.at[i])
        for i, (src, dst) in enumerate(
            (
                (signal_in, signal),
                (filt_in, filt),
                (tokens_in, tokens.at[0]),
                (dft_in, dft),
                (twiddle_in, twiddle),
                (features, feats),
                (weight, weights),
            )
        )
    ]
    for load in loads:
        load.start()

    barrier = pltpu.get_barrier_semaphore()

    def greet(i, carry):
        pl.semaphore_signal(
            barrier, inc=1, device_id={"pos": lax.rem(me + i, blocks)}, device_id_type=MESH
        )
        return carry

    lax.fori_loop(1, blocks, greet, 0)
    for i in range(1, ys):
        there = z_here * ys + lax.rem(y_here + i, ys)
        pl.semaphore_signal(barrier, inc=1, device_id={"chan": there}, device_id_type=MESH)
    across = (1 - z_here) * ys + y_here
    pl.semaphore_signal(
        barrier, inc=1, device_id={"pos": mirror, "chan": across}, device_id_type=MESH
    )

    def eye(size):
        return (
            lax.broadcasted_iota(jnp.int32, (size, size), 0)
            == lax.broadcasted_iota(jnp.int32, (size, size), 1)
        ).astype(F32).astype(BF16)

    eye_lanes, eye_rows = eye(LANES), eye(rows)

    def flipped(block):
        turned = lax.dot_general(eye_lanes, block, NT, preferred_element_type=F32)
        return turned.astype(BF16)

    loads[0].wait()
    for s in range(strips):
        strip = pl.ds(s * LANES, LANES)
        owners = pl.ds(s * per, per)
        send_x[owners] = flipped(signal[:, strip]).reshape(per, mine, rows)
    pl.semaphore_wait(barrier, (blocks - 1) + (ys - 1) + 1)

    def spread(source, target, slot):
        def one(i, carry):
            there = lax.rem(me + i, blocks)
            pltpu.make_async_remote_copy(
                src_ref=source(there),
                dst_ref=target,
                send_sem=send_sem.at[slot],
                recv_sem=recv_sem.at[slot],
                device_id={"pos": there},
                device_id_type=MESH,
            ).start()
            return carry

        lax.fori_loop(1, blocks, one, 0)

    def all_of(source, target, slot):
        others = pl.ds(0, blocks - 1)
        return pltpu.make_async_remote_copy(
            src_ref=source.at[others],
            dst_ref=target.at[others],
            send_sem=send_sem.at[slot],
            recv_sem=recv_sem.at[slot],
            device_id={"pos": lax.rem(me + 1, blocks)},
            device_id_type=MESH,
        )

    spread(lambda there: send_x.at[there], recv_x.at[me], 0)
    recv_x[me] = send_x[me]
    loads[1].wait()
    for s in range(strips):
        strip = pl.ds(s * LANES, LANES)
        send_f[pl.ds(s * per, per)] = flipped(filt[0, :, strip]).reshape(per, mine, rows)
    spread(lambda there: send_f.at[there], recv_f.at[me], 1)
    recv_f[me] = send_f[me]

    lane = lax.broadcasted_iota(jnp.int32, (1, LANES), 1)

    @pl.when(me == 0)
    def _():
        x_head = signal[0:16, :].astype(F32)
        g_head = filt[1, 0:16, :].astype(F32)
        for t in range(steps):
            row = x_head[0:1] * g_head[t : t + 1]
            for r in range(1, t + 1):
                row = row + x_head[r : r + 1] * g_head[t - r : t - r + 1]
            for s in range(strips):
                part = row[:, s * LANES : (s + 1) * LANES]
                for i in range(per):
                    shift = (t * mine - i * mine) % LANES
                    moved = pltpu.roll(part, shift, 1) if shift else part
                    inside = (lane >= t * mine) & (lane < (t + 1) * mine)
                    before = corr_send[s * per + i] if t else jnp.zeros((1, LANES), F32)
                    corr_send[s * per + i] = jnp.where(inside, moved, before)
        spread(lambda there: corr_send.at[there], corr_recv, 2)
        corr_recv[...] = corr_send[0]

    for s in range(strips):
        strip = pl.ds(s * LANES, LANES)
        turned = flipped(filt[1, :, strip]).reshape(per, chunks, GROUP, rows)
        for k in range(chunks):
            send_g[k, pl.ds(s * per, per)] = turned[:, k]
    for k in range(chunks):
        recv_g[k, me] = send_g[k, me]
    spread(lambda there: send_g.at[0, there], recv_g.at[0, me], 3)

    loads[2].wait()
    token_copy = pltpu.make_async_remote_copy(
        src_ref=tokens.at[0], dst_ref=tokens.at[1], send_sem=send_sem.at[10], recv_sem=recv_sem.at[10],
        device_id={"pos": mirror}, device_id_type=MESH,
    )
    token_copy.start()
    for load in loads[3:6]:
        load.wait()

    vocab = feats.shape[1]
    same_place = lax.broadcasted_iota(jnp.int32, (samples, samples), 0) == lax.broadcasted_iota(
        jnp.int32, (samples, samples), 1
    )
    for group in range(2):
        if group == 1:
            token_copy.wait_recv()
        for t in range(steps):
            row = tokens[group, t : t + 1, :].astype(F32)
            column = jnp.sum(jnp.where(same_place, row, 0.0), axis=1, keepdims=True).astype(jnp.int32)
            hot = column == lax.broadcasted_iota(jnp.int32, (samples, vocab), 1)
            hot = hot.astype(F32).astype(BF16)
            part = pl.ds((group * steps + t) * samples, samples)
            query[part] = jnp.dot(hot, feats[0], preferred_element_type=F32).astype(BF16)
            own[part] = jnp.dot(hot, feats[1], preferred_element_type=F32) * jnp.dot(
                hot, feats[2], preferred_element_type=F32
            )

    order = frequency_order(blocks)
    half = rows // 2

    def tiles(body):
        def step(i, carry):
            body(pl.ds(pl.multiple_of(i * 8, 8), 8))
            return carry

        lax.fori_loop(0, GROUP // 8, step, 0)

    real, imag = pl.ds(0, half), pl.ds(half, half)

    def forward_tile(same, diff):
        def body(top):
            def put_lower(slot, re, im):
                wave[slot, 0, top, real] = re
                if im is not None:
                    wave[slot, 0, top, imag] = im

            def put_upper(slot, re, im):
                ar = wave[slot, 0, top, real]
                if im is None:
                    ai = im = jnp.zeros_like(re)
                else:
                    ai = wave[slot, 0, top, imag]
                br, bi = spin((re, im), order[slot], 4 * blocks, -1)
                for part, (vr, vi) in enumerate(((ar + br, ai + bi), (ar - br, ai - bi))):
                    c, s = twiddle[slot, 2 * part], twiddle[slot, 2 * part + 1]
                    wave[slot, part, top, real] = vr * c - vi * s
                    wave[slot, part, top, imag] = vr * s + vi * c

            for across, put in ((real, put_lower), (imag, put_upper)):
                outer_forward(
                    blocks,
                    lambda n, across=across: work[same, n, top, across],
                    lambda n, across=across: work[diff, n, top, across],
                    put,
                )

        return body

    def backward_tile(top):
        def take_lower(slot):
            turned = []
            for part in range(2):
                c, s = twiddle[slot, 2 * part], twiddle[slot, 2 * part + 1]
                re, im = wave[slot, part, top, real], wave[slot, part, top, imag]
                turned.append((re * c + im * s, im * c - re * s))
            (er, ei), (vr, vi) = turned
            br, bi = spin((er - vr, ei - vi), order[slot], 4 * blocks, 1)
            wave[slot, 0, top, real] = br
            wave[slot, 0, top, imag] = bi
            return er + vr, ei + vi

        def take_upper(slot):
            return wave[slot, 0, top, real], wave[slot, 0, top, imag]

        for across, take in ((real, take_lower), (imag, take_upper)):

            def put(n, value, across=across):
                work[0, n, top, across] = value

            outer_backward(blocks, take, put)

    group = max(g for g in range(1, 12) if slots % g == 0)

    def split(value):
        high = value.astype(BF16)
        return high, (value - high.astype(F32)).astype(BF16)

    def inner(value, table):
        high, low = split(value)
        dot = functools.partial(jnp.dot, preferred_element_type=F32)
        return dot(high, dft[table]) + dot(low, dft[table]) + dot(high, dft[table + 1])

    def by_slots(body):
        def step(i, carry):
            body(pl.ds(i * group, group))
            return carry

        lax.fori_loop(0, slots // group, step, 0)

    flat = (group * 2 * GROUP, rows)
    deep = (group, 2, GROUP, rows)

    all_of(send_x, recv_x, 0).wait_recv()
    for k in range(chunks):
        part = pl.ds(k * GROUP, GROUP)

        def widen(n, carry):
            work[0, n] = recv_x[n, part, :].astype(F32)
            return carry

        lax.fori_loop(0, blocks, widen, 0)
        tiles(forward_tile(0, 0))

        def to_spectrum(which, k=k):
            spec_x[k, which] = inner(wave[which].reshape(flat), 0).reshape(deep)

        by_slots(to_spectrum)

    row_id = lax.broadcasted_iota(jnp.int32, (rows, rows), 0)
    col_id = lax.broadcasted_iota(jnp.int32, (rows, rows), 1)
    bundle = 8 if blocks % 8 == 0 else blocks
    for t in range(steps):
        back = ((row_id + col_id == t) | (row_id + col_id == t + rows)).astype(F32).astype(BF16)

        def reverse(i, carry, t=t, back=back):
            which = pl.ds(i * bundle, bundle)
            taken = recv_x[which].reshape(bundle * mine, rows)
            turned = jnp.dot(taken, back, preferred_element_type=F32).astype(BF16)
            shifted[t, which] = turned.reshape(bundle, mine, rows)
            return carry

        lax.fori_loop(0, blocks // bundle, reverse, 0)

    all_of(send_f, recv_f, 1).wait_recv()
    lanes_here = lax.broadcasted_iota(jnp.int32, (mine, LANES), 1)

    def add_block(n, sums, first):
        near = recv_f[blocks - 1 - n].astype(F32)
        if not first:
            far = recv_f[blocks - n, :, 0:LANES].astype(F32)
        result = []
        for t in range(steps):
            x = shifted[t, n].astype(F32)
            other = jnp.zeros((mine, LANES), F32) if first else far
            total = x[:, 0:LANES] * jnp.where(lanes_here > t, near[:, 0:LANES], other)
            for h in range(1, rows // LANES):
                total = total + x[:, h * LANES : (h + 1) * LANES] * near[:, h * LANES : (h + 1) * LANES]
            result.append(sums[t] + total)
        return tuple(result)

    sums = add_block(0, tuple(jnp.zeros((mine, LANES), F32) for _ in range(steps)), True)
    sums = lax.fori_loop(1, blocks, lambda n, c: add_block(n, c, False), sums)
    channel = lax.broadcasted_iota(jnp.int32, (mine, LANES), 0)
    head = recv_f[0, :, 0:LANES].astype(F32)
    seed_rows = jnp.zeros((mine, LANES), F32)
    head_rows = jnp.zeros((mine, LANES), F32)
    for t in range(steps):
        place = lanes_here == t * mine + channel
        seed_rows += jnp.where(place, jnp.sum(sums[t], axis=1, keepdims=True), 0.0)
        value = jnp.sum(jnp.where(lanes_here == t, head, 0.0), axis=1, keepdims=True)
        head_rows += jnp.where(place, value, 0.0)

    @pl.when(me != 0)
    def _():
        pltpu.make_async_remote_copy(
            src_ref=corr_send.at[0], dst_ref=corr_recv, send_sem=send_sem.at[2],
            recv_sem=recv_sem.at[2], device_id={"pos": 0}, device_id_type=MESH,
        ).wait_recv()

    seed_row = jnp.sum(seed_rows, axis=0, keepdims=True) + corr_recv[...]
    seed_send[:, 0:LANES] = seed_row.astype(BF16).astype(F32)
    seed_send[:, LANES : 2 * LANES] = jnp.sum(head_rows, axis=0, keepdims=True)
    spread(lambda there: seed_send, seed_recv.at[me], 4)
    seed_recv[me] = seed_send[...]
    for k in range(1, chunks):
        spread(lambda there, k=k: send_g.at[k, there], recv_g.at[k, me], 3 + 2 * k)

    def convolve(k):
        slot = 3 + 2 * k
        all_of(send_g.at[k], recv_g.at[k], slot).wait_recv()
        part = pl.ds(k * GROUP, GROUP)

        def widen(n, carry):
            early, late = recv_f[n, part, :].astype(F32), recv_g[k, n].astype(F32)
            work[0, n] = early + late
            work[1, n] = early - late
            return carry

        lax.fori_loop(0, blocks, widen, 0)
        tiles(forward_tile(0, 1))

        def through(which):
            h = inner(wave[which].reshape(flat), 0)
            x = spec_x[k, which].reshape(flat)
            hr, hi, xr, xi = h[:, :half], h[:, half:], x[:, :half], x[:, half:]
            spec_h[:, real] = hr * xr - hi * xi
            spec_h[:, imag] = hr * xi + hi * xr
            wave[which] = inner(spec_h[...], 2).reshape(deep)

        by_slots(through)
        tiles(backward_tile)

        def narrow(n, carry):
            send_o[n, k] = work[0, n].astype(BF16)
            return carry

        lax.fori_loop(0, blocks, narrow, 0)
        spread(lambda there: send_o.at[there, k], recv_o.at[me, k], 6 + 2 * k)
        recv_o[me, k] = send_o[me, k]

    def decode():
        all_of(seed_recv, seed_recv, 4).wait_recv()
        which = lax.broadcasted_iota(jnp.int32, (blocks, LANES), 1) // mine
        mod = lax.rem(lax.broadcasted_iota(jnp.int32, (blocks, LANES), 0), per)
        pick = (
            lax.broadcasted_iota(jnp.int32, (strips, blocks), 1) // per
            == lax.broadcasted_iota(jnp.int32, (strips, blocks), 0)
        ).astype(F32).astype(BF16)
        for part in range(2):
            taken = seed_recv[:, 0, part * LANES : (part + 1) * LANES]
            for t in range(steps):
                lined = jnp.zeros((blocks, LANES), F32)
                for i in range(per):
                    shift = ((i - t) * mine) % LANES
                    moved = pltpu.roll(taken, shift, 1) if shift else taken
                    lined = jnp.where((which == i) & (mod == i), moved, lined)
                rows_held[part * steps + t] = jnp.dot(
                    pick, lined.astype(BF16), preferred_element_type=F32
                )
        loads[6].wait()

        count = steps * samples
        for group in (1, 0):
            base = group * count
            for s in range(strips):
                strip = pl.ds(s * LANES, LANES)
                for t in range(steps):
                    total = jnp.broadcast_to(rows_held[t, s : s + 1, :], (samples, LANES))
                    for r in range(t + 1):
                        lag = rows_held[steps + t - r, s : s + 1, :]
                        total = total + lag * own[pl.ds(base + r * samples, samples), strip]
                    part = pl.ds(base + t * samples, samples)
                    gated[part, strip] = (query[part, strip].astype(F32) * total).astype(BF16)
            z = z_here if group == 0 else 1 - z_here

            def product(y, z=z, base=base):
                start = pl.multiple_of((z * ys + y) * columns, LANES)
                return jnp.dot(
                    gated[pl.ds(base, count)], weights[:, pl.ds(start, columns)],
                    preferred_element_type=F32,
                )

            def to_y(i, carry, group=group):
                there = lax.rem(y_here + i, ys)
                part_send[group, there] = product(there).astype(BF16)
                pltpu.make_async_remote_copy(
                    src_ref=part_send.at[group, there], dst_ref=part_recv.at[group, y_here],
                    send_sem=send_sem.at[7 + 4 * group], recv_sem=recv_sem.at[7 + 4 * group],
                    device_id={"chan": z_here * ys + there}, device_id_type=MESH,
                ).start()
                return carry

            lax.fori_loop(1, ys, to_y, 0)
            part_own[group] = product(y_here)

    others = pl.ds(0, ys - 1)
    y_all = [
        pltpu.make_async_remote_copy(
            src_ref=part_send.at[group, others], dst_ref=part_recv.at[group, others],
            send_sem=send_sem.at[7 + 4 * group], recv_sem=recv_sem.at[7 + 4 * group],
            device_id={"chan": z_here * ys + lax.rem(y_here + 1, ys)}, device_id_type=MESH,
        )
        for group in range(2)
    ]
    z_copy = pltpu.make_async_remote_copy(
        src_ref=last_send, dst_ref=last_recv, send_sem=send_sem.at[9], recv_sem=recv_sem.at[9],
        device_id={"pos": mirror, "chan": across}, device_id_type=MESH,
    )

    def add_y(group):
        def one(i, carry):
            part_own[group] += part_recv[group, lax.rem(y_here + i, ys)].astype(F32)
            return carry

        y_all[group].wait_recv()
        lax.fori_loop(1, ys, one, 0)

    decode()
    for k in range(chunks):
        convolve(k)
        if k == 0:
            add_y(1)
            last_send[...] = part_own[1].astype(BF16)
            z_copy.start()

    add_y(0)
    z_copy.wait_recv()
    result = (part_own[0] + last_recv[...].astype(F32)).astype(BF16)
    decoded[...] = result.reshape(steps, samples, columns)

    for k in range(chunks):
        all_of(send_o.at[:, k], recv_o.at[:, k], 6 + 2 * k).wait_recv()
    for s in range(strips):
        taken = recv_o[pl.ds(s * per, per)].reshape(LANES, rows)
        turned = lax.dot_general(eye_rows, taken, NT, preferred_element_type=F32)
        contrib[:, pl.ds(s * LANES, LANES)] = turned.astype(BF16)

    all_of(send_x, recv_x, 0).wait_send()
    all_of(send_f, recv_f, 1).wait_send()

    @pl.when(me == 0)
    def _():
        all_of(corr_send, corr_send, 2).wait_send()

    for k in range(chunks):
        all_of(send_g.at[k], recv_g.at[k], 3 + 2 * k).wait_send()
        all_of(send_o.at[:, k], recv_o.at[:, k], 6 + 2 * k).wait_send()
    all_of(seed_recv, seed_recv, 4).wait_send()
    token_copy.wait_send()
    for copy in y_all:
        copy.wait_send()
    z_copy.wait_send()


def per_device(chans, prompt_signal, long_filter, sample_tokens, token_features, out_weight):
    blocks = lax.axis_size("pos")
    rows, width = prompt_signal.shape
    samples, steps = sample_tokens.shape
    mine = width // blocks
    slots = blocks + 1
    chunks = mine // GROUP
    zs = 2
    ys = chans // zs
    columns = out_weight.shape[1] // chans
    twiddle, dft = tables(blocks, rows)
    group = max(g for g in range(1, 12) if slots % g == 0)
    vmem, dma = pltpu.VMEM, pltpu.SemaphoreType.DMA
    by_vmem = pl.BlockSpec(memory_space=pltpu.VMEM)
    by_hbm = pl.BlockSpec(memory_space=pl.ANY)
    count = steps * samples
    contributions, decoded = pl.pallas_call(
        functools.partial(kernel, blocks, chans, zs),
        out_shape=(
            jax.ShapeDtypeStruct((rows, width), BF16),
            jax.ShapeDtypeStruct((steps, samples, columns), BF16),
        ),
        in_specs=[by_hbm] * 7,
        out_specs=(by_vmem, by_vmem),
        scratch_shapes=[
            vmem(prompt_signal.shape, BF16),
            vmem(long_filter.shape, BF16),
            vmem((2, steps, samples), jnp.int32),
            vmem((blocks, mine, rows), BF16),
            vmem((blocks, mine, rows), BF16),
            vmem((chunks, blocks, GROUP, rows), BF16),
            vmem((blocks, mine, rows), BF16),
            vmem((blocks, mine, rows), BF16),
            vmem((chunks, blocks, GROUP, rows), BF16),
            vmem((blocks, chunks, GROUP, rows), BF16),
            vmem((blocks, chunks, GROUP, rows), BF16),
            vmem((2, blocks, GROUP, rows), F32),
            vmem((slots, 2, GROUP, rows), F32),
            vmem((chunks, slots, 2, GROUP, rows), F32),
            vmem((group * 2 * GROUP, rows), F32),
            vmem((steps, blocks, mine, rows), BF16),
            vmem((blocks, 1, LANES), F32),
            vmem((1, LANES), F32),
            vmem((1, 2 * LANES), F32),
            vmem((blocks, 1, 2 * LANES), F32),
            vmem((2 * steps, width // LANES, LANES), F32),
            vmem((3, token_features.shape[0], width), BF16),
            vmem(out_weight.shape, BF16),
            vmem(twiddle.shape, F32),
            vmem(dft.shape, BF16),
            vmem((2 * count, width), BF16),
            vmem((2 * count, width), F32),
            vmem((2 * count, width), BF16),
            vmem((2, ys, count, columns), BF16),
            vmem((2, ys, count, columns), BF16),
            vmem((2, count, columns), F32),
            vmem((count, columns), BF16),
            vmem((count, columns), BF16),
            dma((7,)),
            dma((12,)),
            dma((12,)),
        ],
        compiler_params=pltpu.CompilerParams(
            collective_id=0, has_side_effects=True, vmem_limit_bytes=50 * 2**20
        ),
        name="conv_decode",
    )(
        prompt_signal,
        long_filter,
        sample_tokens.T,
        jnp.transpose(token_features, (1, 0, 2)),
        out_weight,
        jnp.asarray(twiddle),
        jnp.asarray(dft),
    )
    return contributions, jnp.transpose(decoded, (1, 0, 2))


def solution(mesh):
    placed = (
        P("pos", "chan"),
        P(None, "pos", "chan"),
        P("pos", None),
        P(None, None, "chan"),
        P("chan", None),
    )
    return jax.shard_map(
        functools.partial(per_device, mesh.shape["chan"]),
        mesh=mesh,
        in_specs=placed,
        out_specs=(P("pos", "chan"), P("pos", None, "chan")),
        check_vma=False,
    )
```

```python
import functools
import math

import jax
import jax.numpy as jnp
import numpy as np
from jax import lax
from jax.experimental import pallas as pl
from jax.experimental.pallas import tpu as pltpu
from jax.sharding import PartitionSpec as P

MESH = pl.DeviceIdType.MESH
LANES = 128
GROUP = 16
F32 = jnp.float32
BF16 = jnp.bfloat16
NT = (((1,), (1,)), ((), ()))


def turn(value, cosine, sine):
    re, im = value
    near = lambda a, b: abs(a - b) < 1e-12
    if near(sine, 0.0):
        return (re, im) if cosine > 0 else (-re, -im)
    if near(cosine, 0.0):
        return (-im, re) if sine > 0 else (im, -re)
    if near(abs(cosine), abs(sine)):
        scale = abs(cosine)
        a, b = math.copysign(1, cosine), math.copysign(1, sine)
        if a > 0:
            return ((re - im if b > 0 else re + im) * scale, (im + re if b > 0 else im - re) * scale)
        return ((re + im if b > 0 else re - im) * -scale, (im - re if b > 0 else im + re) * -scale)
    return (re * cosine - im * sine, re * sine + im * cosine)


def spin(value, index, period, sign):
    angle = 2.0 * math.pi * index / period
    return turn(value, math.cos(angle), sign * math.sin(angle))


def fft(values, sign):
    size = len(values)
    if size == 1:
        return values
    even, odd = fft(values[::2], sign), fft(values[1::2], sign)
    low, high = [], []
    for k in range(size // 2):
        (er, ei), (tr, ti) = even[k], spin(odd[k], k, size, sign)
        low.append((er + tr, ei + ti))
        high.append((er - tr, ei - ti))
    return low + high


def frequency_order(blocks):
    order = [4 * q + 1 for q in range(blocks // 2)]
    size, factor = blocks, 2
    while size >= 4:
        order += [factor * (4 * q + 1) for q in range(size // 4)]
        size, factor = size // 2, factor * 2
    return order + [0, blocks]


def outer_forward(blocks, same, diff, put):
    half = blocks // 2
    held = [spin((diff(n), -diff(n + half)), n, 2 * blocks, -1) for n in range(half)]
    slot = 0
    for re, im in fft(held, -1):
        put(slot, re, im)
        slot += 1
    size = blocks
    real = [(same(n), same(n + half)) for n in range(half)]
    while size >= 4:
        half, quarter = size // 2, size // 4
        lower = [a + b for a, b in real]
        away = [a - b for a, b in real]
        held = [spin((away[n], -away[n + quarter]), n, size, -1) for n in range(quarter)]
        for re, im in fft(held, -1):
            put(slot, re, im)
            slot += 1
        real = [(lower[n], lower[n + quarter]) for n in range(quarter)]
        size = half
    first, second = real[0]
    put(slot, first + second, None)
    put(slot + 1, first - second, None)


def outer_backward(blocks, take, put):
    first, last = take(blocks - 1)[0] * 0.5, take(blocks)[0] * 0.5
    real = [first + last, first - last]
    size, start = 4, blocks - 2
    while size <= blocks:
        quarter = size // 4
        back = fft([take(start + q) for q in range(quarter)], 1)
        back = [spin(value, n, size, 1) for n, value in enumerate(back)]
        wave = [re for re, _ in back] + [-im for _, im in back]
        real = [a + b for a, b in zip(real, wave)] + [a - b for a, b in zip(real, wave)]
        size, start = size * 2, start - size // 2
    half = blocks // 2
    back = fft([take(q) for q in range(half)], 1)
    for n, value in enumerate(back):
        re, im = spin(value, n, 2 * blocks, 1)
        put(n, real[n] - re)
        put(n + half, real[n + half] + im)


def tables(blocks, rows):
    order = np.array(frequency_order(blocks))
    length, half = 2 * blocks * rows, rows // 2
    inner = np.arange(half)
    angle = 2.0 * np.pi * (order[:, None] * inner[None, :] % length) / length
    odd = angle + 2.0 * np.pi * inner[None, :] / rows
    twiddle = np.stack([np.cos(angle), -np.sin(angle), np.cos(odd), -np.sin(odd)], 1)
    twiddle = np.repeat(twiddle.astype(np.float32)[:, :, None, :], 8, 2)
    angle = 2.0 * np.pi * (inner[:, None] * inner[None, :] % half) / half
    cosine, sine = np.cos(angle), np.sin(angle)
    forward = np.block([[cosine, -sine], [sine, cosine]]).astype(np.float32)
    backward = (forward.T / (blocks * rows)).astype(np.float32)

    def split(table):
        high = table.astype(jnp.bfloat16)
        return [high, (table - high.astype(np.float32)).astype(jnp.bfloat16)]

    return twiddle, np.stack(split(forward) + split(backward))


def kernel(
    blocks, chans, zs, signal_in, filt_in, tokens_in, features, weight, twiddle_in, dft_in,
    contrib, decoded,
    signal, filt, tokens,
    send_x, send_f, send_g, recv_x, recv_f, recv_g, send_o, recv_o,
    work, wave, spec_x, spec_h, shifted, reversal,
    corr_send, corr_recv, seed_send, seed_recv, rows_held,
    feats, weights, twiddle, dft, query, own, gated,
    part_send, part_recv, part_own, last_send, last_recv,
    local_sem, send_sem, recv_sem,
):
    me, chan = lax.axis_index("pos"), lax.axis_index("chan")
    rows, width = signal.shape
    mine = width // blocks
    slots = blocks + 1
    chunks = mine // GROUP
    per = LANES // mine
    strips = width // LANES
    ys = chans // zs
    z_here, y_here = chan // ys, lax.rem(chan, ys)
    planes = blocks // 4
    mirror = (3 - me // planes) * planes + lax.rem(me, planes)
    steps = tokens.shape[1]
    samples = tokens.shape[2]
    columns = decoded.shape[2]

    loads = [
        pltpu.make_async_copy(src, dst, local_sem.at[i])
        for i, (src, dst) in enumerate(
            (
                (signal_in, signal),
                (filt_in, filt),
                (tokens_in, tokens.at[0]),
                (dft_in, dft),
                (twiddle_in, twiddle),
                (features, feats),
                (weight, weights),
            )
        )
    ]
    barrier = pltpu.get_barrier_semaphore()

    def greet(i, carry):
        pl.semaphore_signal(
            barrier, inc=1, device_id={"pos": lax.rem(me + i, blocks)}, device_id_type=MESH
        )
        return carry

    lax.fori_loop(1, blocks, greet, 0)
    for i in range(1, ys):
        there = z_here * ys + lax.rem(y_here + i, ys)
        pl.semaphore_signal(barrier, inc=1, device_id={"chan": there}, device_id_type=MESH)
    across = (1 - z_here) * ys + y_here
    pl.semaphore_signal(
        barrier, inc=1, device_id={"pos": mirror, "chan": across}, device_id_type=MESH
    )

    loads[0].start()

    def eye(size):
        return (
            lax.broadcasted_iota(jnp.int32, (size, size), 0)
            == lax.broadcasted_iota(jnp.int32, (size, size), 1)
        ).astype(F32).astype(BF16)

    eye_lanes, eye_rows = eye(LANES), eye(rows)

    def flipped(block):
        turned = lax.dot_general(eye_lanes, block, NT, preferred_element_type=F32)
        return turned.astype(BF16)

    loads[0].wait()
    for load in loads[1:]:
        load.start()
    row_id = lax.broadcasted_iota(jnp.int32, (rows, rows), 0)
    col_id = lax.broadcasted_iota(jnp.int32, (rows, rows), 1)
    for t in range(steps):
        back = (row_id + col_id == t) | (row_id + col_id == t + rows)
        reversal[:, t * rows : (t + 1) * rows] = back.astype(F32).astype(BF16)
    for s in range(strips):
        strip = pl.ds(s * LANES, LANES)
        owners = pl.ds(s * per, per)
        send_x[owners] = flipped(signal[:, strip]).reshape(per, mine, rows)
    pl.semaphore_wait(barrier, (blocks - 1) + (ys - 1) + 1)

    def spread(source, target, slot, start=1, stop=blocks, sent=None):
        def one(i, carry):
            there = lax.rem(me + i, blocks)
            pltpu.make_async_remote_copy(
                src_ref=source(there),
                dst_ref=target,
                send_sem=send_sem.at[slot if sent is None else sent],
                recv_sem=recv_sem.at[slot],
                device_id={"pos": there},
                device_id_type=MESH,
            ).start()
            return carry

        lax.fori_loop(start, stop, one, 0)

    def all_of(source, target, slot, count=blocks - 1):
        others = pl.ds(0, count)
        return pltpu.make_async_remote_copy(
            src_ref=source.at[others],
            dst_ref=target.at[others],
            send_sem=send_sem.at[slot],
            recv_sem=recv_sem.at[slot],
            device_id={"pos": lax.rem(me + 1, blocks)},
            device_id_type=MESH,
        )

    ahead = max(blocks // 4, 1)
    low = blocks // 2 - ahead // 2
    high = low + ahead

    def spread_ahead(source, target, slot, sent):
        spread(source, target, slot, low, high, sent)

    def spread_rest(source, target, slot):
        spread(source, target, slot, 1, low)
        spread(source, target, slot, high, blocks)

    def rest_of(source, target, slot):
        return all_of(source, target, slot, blocks - 1 - ahead)

    def ahead_of(source, target, sent):
        return all_of(source, target, sent, ahead)

    spread(lambda there: send_x.at[there], recv_x.at[me], 0)
    recv_x[me] = send_x[me]
    loads[1].wait()
    for s in range(strips):
        strip = pl.ds(s * LANES, LANES)
        send_f[pl.ds(s * per, per)] = flipped(filt[0, :, strip]).reshape(per, mine, rows)
    spread_ahead(lambda there: send_f.at[there], recv_f.at[me], 1, 12)
    recv_f[me] = send_f[me]

    lane = lax.broadcasted_iota(jnp.int32, (1, LANES), 1)

    @pl.when(me == 0)
    def _():
        x_head = signal[0:16, :].astype(F32)
        g_head = filt[1, 0:16, :].astype(F32)
        for t in range(steps):
            row = x_head[0:1] * g_head[t : t + 1]
            for r in range(1, t + 1):
                row = row + x_head[r : r + 1] * g_head[t - r : t - r + 1]
            for s in range(strips):
                part = row[:, s * LANES : (s + 1) * LANES]
                for i in range(per):
                    shift = (t * mine - i * mine) % LANES
                    moved = pltpu.roll(part, shift, 1) if shift else part
                    inside = (lane >= t * mine) & (lane < (t + 1) * mine)
                    before = corr_send[s * per + i] if t else jnp.zeros((1, LANES), F32)
                    corr_send[s * per + i] = jnp.where(inside, moved, before)
        spread(lambda there: corr_send.at[there], corr_recv, 2)
        corr_recv[...] = corr_send[0]

    for s in range(strips):
        strip = pl.ds(s * LANES, LANES)
        turned = flipped(filt[1, :, strip]).reshape(per, chunks, GROUP, rows)
        for k in range(chunks):
            send_g[k, pl.ds(s * per, per)] = turned[:, k]
    for k in range(chunks):
        recv_g[k, me] = send_g[k, me]

    loads[2].wait()
    token_copy = pltpu.make_async_remote_copy(
        src_ref=tokens.at[0], dst_ref=tokens.at[1], send_sem=send_sem.at[10], recv_sem=recv_sem.at[10],
        device_id={"pos": mirror}, device_id_type=MESH,
    )
    token_copy.start()
    for load in loads[3:6]:
        load.wait()

    vocab = feats.shape[1]
    same_place = lax.broadcasted_iota(jnp.int32, (samples, samples), 0) == lax.broadcasted_iota(
        jnp.int32, (samples, samples), 1
    )
    for group in range(2):
        if group == 1:
            token_copy.wait_recv()
        for t in range(steps):
            row = tokens[group, t : t + 1, :].astype(F32)
            column = jnp.sum(jnp.where(same_place, row, 0.0), axis=1, keepdims=True).astype(jnp.int32)
            hot = column == lax.broadcasted_iota(jnp.int32, (samples, vocab), 1)
            hot = hot.astype(F32).astype(BF16)
            part = pl.ds((group * steps + t) * samples, samples)
            query[part] = jnp.dot(hot, feats[0], preferred_element_type=F32).astype(BF16)
            own[part] = jnp.dot(hot, feats[1], preferred_element_type=F32) * jnp.dot(
                hot, feats[2], preferred_element_type=F32
            )

    order = frequency_order(blocks)
    half = rows // 2

    def tiles(body):
        def step(i, carry):
            body(pl.ds(pl.multiple_of(i * 8, 8), 8))
            return carry

        lax.fori_loop(0, GROUP // 8, step, 0)

    real, imag = pl.ds(0, half), pl.ds(half, half)

    def forward_tile(same, diff):
        def body(top):
            def put_lower(slot, re, im):
                wave[slot, 0, top, real] = re
                if im is not None:
                    wave[slot, 0, top, imag] = im

            def put_upper(slot, re, im):
                ar = wave[slot, 0, top, real]
                if im is None:
                    ai = im = jnp.zeros_like(re)
                else:
                    ai = wave[slot, 0, top, imag]
                br, bi = spin((re, im), order[slot], 4 * blocks, -1)
                for part, (vr, vi) in enumerate(((ar + br, ai + bi), (ar - br, ai - bi))):
                    c, s = twiddle[slot, 2 * part], twiddle[slot, 2 * part + 1]
                    wave[slot, part, top, real] = vr * c - vi * s
                    wave[slot, part, top, imag] = vr * s + vi * c

            for across, put in ((real, put_lower), (imag, put_upper)):
                outer_forward(
                    blocks,
                    lambda n, across=across: work[same, n, top, across],
                    lambda n, across=across: work[diff, n, top, across],
                    put,
                )

        return body

    def backward_tile(top):
        def take_lower(slot):
            turned = []
            for part in range(2):
                c, s = twiddle[slot, 2 * part], twiddle[slot, 2 * part + 1]
                re, im = wave[slot, part, top, real], wave[slot, part, top, imag]
                turned.append((re * c + im * s, im * c - re * s))
            (er, ei), (vr, vi) = turned
            br, bi = spin((er - vr, ei - vi), order[slot], 4 * blocks, 1)
            wave[slot, 0, top, real] = br
            wave[slot, 0, top, imag] = bi
            return er + vr, ei + vi

        def take_upper(slot):
            return wave[slot, 0, top, real], wave[slot, 0, top, imag]

        for across, take in ((real, take_lower), (imag, take_upper)):

            def put(n, value, across=across):
                work[0, n, top, across] = value

            outer_backward(blocks, take, put)

    group = max(g for g in range(1, 12) if slots % g == 0)

    def split(value):
        high = value.astype(BF16)
        return high, (value - high.astype(F32)).astype(BF16)

    def inner(value, table):
        high, low = split(value)
        dot = functools.partial(jnp.dot, preferred_element_type=F32)
        return dot(high, dft[table]) + dot(low, dft[table]) + dot(high, dft[table + 1])

    def by_slots(body):
        def step(i, carry):
            body(pl.ds(i * group, group))
            return carry

        lax.fori_loop(0, slots // group, step, 0)

    flat = (group * 2 * GROUP, rows)
    deep = (group, 2, GROUP, rows)

    all_of(send_x, recv_x, 0).wait_send()
    spread_rest(lambda there: send_f.at[there], recv_f.at[me], 1)
    spread_ahead(lambda there: send_g.at[0, there], recv_g.at[0, me], 3, 13)

    all_of(send_x, recv_x, 0).wait_recv()
    bundle = 8 if blocks % 8 == 0 else blocks

    def reverse(i, carry):
        which = pl.ds(i * bundle, bundle)
        taken = recv_x[which].reshape(bundle * mine, rows)
        turned = jnp.dot(taken, reversal[...], preferred_element_type=F32).astype(BF16)
        for t in range(steps):
            part = turned[:, t * rows : (t + 1) * rows]
            shifted[t, which] = part.reshape(bundle, mine, rows)
        return carry

    lax.fori_loop(0, blocks // bundle, reverse, 0)
    for k in range(chunks):
        part = pl.ds(k * GROUP, GROUP)

        def widen(n, carry):
            work[0, n] = recv_x[n, part, :].astype(F32)
            return carry

        lax.fori_loop(0, blocks, widen, 0)
        tiles(forward_tile(0, 0))

        def to_spectrum(which, k=k):
            spec_x[k, which] = inner(wave[which].reshape(flat), 0).reshape(deep)

        by_slots(to_spectrum)

    rest_of(send_f, recv_f, 1).wait_send()
    spread_rest(lambda there: send_g.at[0, there], recv_g.at[0, me], 3)
    all_of(send_f, recv_f, 1).wait_recv()
    lanes_here = lax.broadcasted_iota(jnp.int32, (mine, LANES), 1)

    def add_block(n, sums, first):
        near = recv_f[blocks - 1 - n].astype(F32)
        if not first:
            far = recv_f[blocks - n, :, 0:LANES].astype(F32)
        result = []
        for t in range(steps):
            x = shifted[t, n].astype(F32)
            other = jnp.zeros((mine, LANES), F32) if first else far
            total = x[:, 0:LANES] * jnp.where(lanes_here > t, near[:, 0:LANES], other)
            for h in range(1, rows // LANES):
                total = total + x[:, h * LANES : (h + 1) * LANES] * near[:, h * LANES : (h + 1) * LANES]
            result.append(sums[t] + total)
        return tuple(result)

    sums = add_block(0, tuple(jnp.zeros((mine, LANES), F32) for _ in range(steps)), True)
    sums = lax.fori_loop(1, blocks, lambda n, c: add_block(n, c, False), sums)
    channel = lax.broadcasted_iota(jnp.int32, (mine, LANES), 0)
    head = recv_f[0, :, 0:LANES].astype(F32)
    seed_rows = jnp.zeros((mine, LANES), F32)
    head_rows = jnp.zeros((mine, LANES), F32)
    for t in range(steps):
        place = lanes_here == t * mine + channel
        seed_rows += jnp.where(place, jnp.sum(sums[t], axis=1, keepdims=True), 0.0)
        value = jnp.sum(jnp.where(lanes_here == t, head, 0.0), axis=1, keepdims=True)
        head_rows += jnp.where(place, value, 0.0)

    @pl.when(me != 0)
    def _():
        pltpu.make_async_remote_copy(
            src_ref=corr_send.at[0], dst_ref=corr_recv, send_sem=send_sem.at[2],
            recv_sem=recv_sem.at[2], device_id={"pos": 0}, device_id_type=MESH,
        ).wait_recv()

    seed_row = jnp.sum(seed_rows, axis=0, keepdims=True) + corr_recv[...]
    seed_send[:, 0:LANES] = seed_row.astype(BF16).astype(F32)
    seed_send[:, LANES : 2 * LANES] = jnp.sum(head_rows, axis=0, keepdims=True)
    spread(lambda there: seed_send, seed_recv.at[me], 4)
    seed_recv[me] = seed_send[...]
    for k in range(1, chunks):
        spread(lambda there, k=k: send_g.at[k, there], recv_g.at[k, me], 3 + 2 * k)

    def convolve(k):
        slot = 3 + 2 * k
        all_of(send_g.at[k], recv_g.at[k], slot).wait_recv()
        part = pl.ds(k * GROUP, GROUP)

        def widen(n, carry):
            early, late = recv_f[n, part, :].astype(F32), recv_g[k, n].astype(F32)
            work[0, n] = early + late
            work[1, n] = early - late
            return carry

        lax.fori_loop(0, blocks, widen, 0)
        tiles(forward_tile(0, 1))

        def through(which):
            h = inner(wave[which].reshape(flat), 0)
            x = spec_x[k, which].reshape(flat)
            hr, hi, xr, xi = h[:, :half], h[:, half:], x[:, :half], x[:, half:]
            spec_h[:, real] = hr * xr - hi * xi
            spec_h[:, imag] = hr * xi + hi * xr
            wave[which] = inner(spec_h[...], 2).reshape(deep)

        by_slots(through)
        tiles(backward_tile)

        def narrow(n, carry):
            send_o[n, k] = work[0, n].astype(BF16)
            return carry

        lax.fori_loop(0, blocks, narrow, 0)
        spread(lambda there: send_o.at[there, k], recv_o.at[me, k], 6 + 2 * k)
        recv_o[me, k] = send_o[me, k]

    def decode():
        all_of(seed_recv, seed_recv, 4).wait_recv()
        which = lax.broadcasted_iota(jnp.int32, (blocks, LANES), 1) // mine
        mod = lax.rem(lax.broadcasted_iota(jnp.int32, (blocks, LANES), 0), per)
        pick = (
            lax.broadcasted_iota(jnp.int32, (strips, blocks), 1) // per
            == lax.broadcasted_iota(jnp.int32, (strips, blocks), 0)
        ).astype(F32).astype(BF16)
        for part in range(2):
            taken = seed_recv[:, 0, part * LANES : (part + 1) * LANES]
            for t in range(steps):
                lined = jnp.zeros((blocks, LANES), F32)
                for i in range(per):
                    shift = ((i - t) * mine) % LANES
                    moved = pltpu.roll(taken, shift, 1) if shift else taken
                    lined = jnp.where((which == i) & (mod == i), moved, lined)
                rows_held[part * steps + t] = jnp.dot(
                    pick, lined.astype(BF16), preferred_element_type=F32
                )
        loads[6].wait()

        count = steps * samples
        for group in (1, 0):
            base = group * count
            for s in range(strips):
                strip = pl.ds(s * LANES, LANES)
                for t in range(steps):
                    total = jnp.broadcast_to(rows_held[t, s : s + 1, :], (samples, LANES))
                    for r in range(t + 1):
                        lag = rows_held[steps + t - r, s : s + 1, :]
                        total = total + lag * own[pl.ds(base + r * samples, samples), strip]
                    part = pl.ds(base + t * samples, samples)
                    gated[part, strip] = (query[part, strip].astype(F32) * total).astype(BF16)
            z = z_here if group == 0 else 1 - z_here

            def product(y, z=z, base=base):
                start = pl.multiple_of((z * ys + y) * columns, LANES)
                return jnp.dot(
                    gated[pl.ds(base, count)], weights[:, pl.ds(start, columns)],
                    preferred_element_type=F32,
                )

            def to_y(i, carry, group=group):
                there = lax.rem(y_here + i, ys)
                part_send[group, there] = product(there).astype(BF16)
                pltpu.make_async_remote_copy(
                    src_ref=part_send.at[group, there], dst_ref=part_recv.at[group, y_here],
                    send_sem=send_sem.at[7 + 4 * group], recv_sem=recv_sem.at[7 + 4 * group],
                    device_id={"chan": z_here * ys + there}, device_id_type=MESH,
                ).start()
                return carry

            lax.fori_loop(1, ys, to_y, 0)
            part_own[group] = product(y_here)

    others = pl.ds(0, ys - 1)
    y_all = [
        pltpu.make_async_remote_copy(
            src_ref=part_send.at[group, others], dst_ref=part_recv.at[group, others],
            send_sem=send_sem.at[7 + 4 * group], recv_sem=recv_sem.at[7 + 4 * group],
            device_id={"chan": z_here * ys + lax.rem(y_here + 1, ys)}, device_id_type=MESH,
        )
        for group in range(2)
    ]
    z_copy = pltpu.make_async_remote_copy(
        src_ref=last_send, dst_ref=last_recv, send_sem=send_sem.at[9], recv_sem=recv_sem.at[9],
        device_id={"pos": mirror, "chan": across}, device_id_type=MESH,
    )

    def add_y(group):
        def one(i, carry):
            part_own[group] += part_recv[group, lax.rem(y_here + i, ys)].astype(F32)
            return carry

        y_all[group].wait_recv()
        lax.fori_loop(1, ys, one, 0)

    convolve(0)
    decode()
    for k in range(1, chunks):
        convolve(k)
    add_y(1)
    last_send[...] = part_own[1].astype(BF16)
    z_copy.start()
    add_y(0)
    z_copy.wait_recv()
    result = (part_own[0] + last_recv[...].astype(F32)).astype(BF16)
    decoded[...] = result.reshape(steps, samples, columns)

    for k in range(chunks):
        all_of(send_o.at[:, k], recv_o.at[:, k], 6 + 2 * k).wait_recv()
    for s in range(strips):
        taken = recv_o[pl.ds(s * per, per)].reshape(LANES, rows)
        turned = lax.dot_general(eye_rows, taken, NT, preferred_element_type=F32)
        contrib[:, pl.ds(s * LANES, LANES)] = turned.astype(BF16)

    ahead_of(send_f, recv_f, 12).wait_send()
    ahead_of(send_g.at[0], recv_g.at[0], 13).wait_send()
    rest_of(send_g.at[0], recv_g.at[0], 3).wait_send()

    @pl.when(me == 0)
    def _():
        all_of(corr_send, corr_send, 2).wait_send()

    for k in range(chunks):
        if k > 0:
            all_of(send_g.at[k], recv_g.at[k], 3 + 2 * k).wait_send()
        all_of(send_o.at[:, k], recv_o.at[:, k], 6 + 2 * k).wait_send()
    all_of(seed_recv, seed_recv, 4).wait_send()
    token_copy.wait_send()
    for copy in y_all:
        copy.wait_send()
    z_copy.wait_send()


def per_device(chans, prompt_signal, long_filter, sample_tokens, token_features, out_weight):
    blocks = lax.axis_size("pos")
    rows, width = prompt_signal.shape
    samples, steps = sample_tokens.shape
    mine = width // blocks
    slots = blocks + 1
    chunks = mine // GROUP
    zs = 2
    ys = chans // zs
    columns = out_weight.shape[1] // chans
    twiddle, dft = tables(blocks, rows)
    group = max(g for g in range(1, 12) if slots % g == 0)
    vmem, dma = pltpu.VMEM, pltpu.SemaphoreType.DMA
    by_vmem = pl.BlockSpec(memory_space=pltpu.VMEM)
    by_hbm = pl.BlockSpec(memory_space=pl.ANY)
    count = steps * samples
    contributions, decoded = pl.pallas_call(
        functools.partial(kernel, blocks, chans, zs),
        out_shape=(
            jax.ShapeDtypeStruct((rows, width), BF16),
            jax.ShapeDtypeStruct((steps, samples, columns), BF16),
        ),
        in_specs=[by_hbm] * 7,
        out_specs=(by_vmem, by_vmem),
        scratch_shapes=[
            vmem(prompt_signal.shape, BF16),
            vmem(long_filter.shape, BF16),
            vmem((2, steps, samples), jnp.int32),
            vmem((blocks, mine, rows), BF16),
            vmem((blocks, mine, rows), BF16),
            vmem((chunks, blocks, GROUP, rows), BF16),
            vmem((blocks, mine, rows), BF16),
            vmem((blocks, mine, rows), BF16),
            vmem((chunks, blocks, GROUP, rows), BF16),
            vmem((blocks, chunks, GROUP, rows), BF16),
            vmem((blocks, chunks, GROUP, rows), BF16),
            vmem((2, blocks, GROUP, rows), F32),
            vmem((slots, 2, GROUP, rows), F32),
            vmem((chunks, slots, 2, GROUP, rows), F32),
            vmem((group * 2 * GROUP, rows), F32),
            vmem((steps, blocks, mine, rows), BF16),
            vmem((rows, steps * rows), BF16),
            vmem((blocks, 1, LANES), F32),
            vmem((1, LANES), F32),
            vmem((1, 2 * LANES), F32),
            vmem((blocks, 1, 2 * LANES), F32),
            vmem((2 * steps, width // LANES, LANES), F32),
            vmem((3, token_features.shape[0], width), BF16),
            vmem(out_weight.shape, BF16),
            vmem(twiddle.shape, F32),
            vmem(dft.shape, BF16),
            vmem((2 * count, width), BF16),
            vmem((2 * count, width), F32),
            vmem((2 * count, width), BF16),
            vmem((2, ys, count, columns), BF16),
            vmem((2, ys, count, columns), BF16),
            vmem((2, count, columns), F32),
            vmem((count, columns), BF16),
            vmem((count, columns), BF16),
            dma((7,)),
            dma((14,)),
            dma((14,)),
        ],
        compiler_params=pltpu.CompilerParams(
            collective_id=0, has_side_effects=True, vmem_limit_bytes=60 * 2**20
        ),
        name="conv_decode",
    )(
        prompt_signal,
        long_filter,
        sample_tokens.T,
        jnp.transpose(token_features, (1, 0, 2)),
        out_weight,
        jnp.asarray(twiddle),
        jnp.asarray(dft),
    )
    return contributions, jnp.transpose(decoded, (1, 0, 2))


def solution(mesh):
    placed = (
        P("pos", "chan"),
        P(None, "pos", "chan"),
        P("pos", None),
        P(None, None, "chan"),
        P("chan", None),
    )
    return jax.shard_map(
        functools.partial(per_device, mesh.shape["chan"]),
        mesh=mesh,
        in_specs=placed,
        out_specs=(P("pos", "chan"), P("pos", None, "chan")),
        check_vma=False,
    )
```

```python
import functools
import math

import jax
import jax.numpy as jnp
import numpy as np
from jax import lax
from jax.experimental import pallas as pl
from jax.experimental.pallas import tpu as pltpu
from jax.sharding import PartitionSpec as P

MESH = pl.DeviceIdType.MESH
LANES = 128
GROUP = 16
F32 = jnp.float32
BF16 = jnp.bfloat16
NT = (((1,), (1,)), ((), ()))


def turn(value, cosine, sine):
    re, im = value
    near = lambda a, b: abs(a - b) < 1e-12
    if near(sine, 0.0):
        return (re, im) if cosine > 0 else (-re, -im)
    if near(cosine, 0.0):
        return (-im, re) if sine > 0 else (im, -re)
    if near(abs(cosine), abs(sine)):
        scale = abs(cosine)
        a, b = math.copysign(1, cosine), math.copysign(1, sine)
        if a > 0:
            return ((re - im if b > 0 else re + im) * scale, (im + re if b > 0 else im - re) * scale)
        return ((re + im if b > 0 else re - im) * -scale, (im - re if b > 0 else im + re) * -scale)
    return (re * cosine - im * sine, re * sine + im * cosine)


def spin(value, index, period, sign):
    angle = 2.0 * math.pi * index / period
    return turn(value, math.cos(angle), sign * math.sin(angle))


def fft(values, sign):
    size = len(values)
    if size == 1:
        return values
    even, odd = fft(values[::2], sign), fft(values[1::2], sign)
    low, high = [], []
    for k in range(size // 2):
        (er, ei), (tr, ti) = even[k], spin(odd[k], k, size, sign)
        low.append((er + tr, ei + ti))
        high.append((er - tr, ei - ti))
    return low + high


def frequency_order(blocks):
    order = [4 * q + 1 for q in range(blocks // 2)]
    size, factor = blocks, 2
    while size >= 4:
        order += [factor * (4 * q + 1) for q in range(size // 4)]
        size, factor = size // 2, factor * 2
    return order + [0, blocks]


def outer_forward(blocks, same, diff, put):
    half = blocks // 2
    held = [spin((diff(n), -diff(n + half)), n, 2 * blocks, -1) for n in range(half)]
    slot = 0
    for re, im in fft(held, -1):
        put(slot, re, im)
        slot += 1
    size = blocks
    real = [(same(n), same(n + half)) for n in range(half)]
    while size >= 4:
        half, quarter = size // 2, size // 4
        lower = [a + b for a, b in real]
        away = [a - b for a, b in real]
        held = [spin((away[n], -away[n + quarter]), n, size, -1) for n in range(quarter)]
        for re, im in fft(held, -1):
            put(slot, re, im)
            slot += 1
        real = [(lower[n], lower[n + quarter]) for n in range(quarter)]
        size = half
    first, second = real[0]
    put(slot, first + second, None)
    put(slot + 1, first - second, None)


def outer_backward(blocks, take, put):
    first, last = take(blocks - 1)[0] * 0.5, take(blocks)[0] * 0.5
    real = [first + last, first - last]
    size, start = 4, blocks - 2
    while size <= blocks:
        quarter = size // 4
        back = fft([take(start + q) for q in range(quarter)], 1)
        back = [spin(value, n, size, 1) for n, value in enumerate(back)]
        wave = [re for re, _ in back] + [-im for _, im in back]
        real = [a + b for a, b in zip(real, wave)] + [a - b for a, b in zip(real, wave)]
        size, start = size * 2, start - size // 2
    half = blocks // 2
    back = fft([take(q) for q in range(half)], 1)
    for n, value in enumerate(back):
        re, im = spin(value, n, 2 * blocks, 1)
        put(n, real[n] - re)
        put(n + half, real[n + half] + im)


def tables(blocks, rows):
    order = np.array(frequency_order(blocks))
    length, half = 2 * blocks * rows, rows // 2
    inner = np.arange(half)
    angle = 2.0 * np.pi * (order[:, None] * inner[None, :] % length) / length
    odd = angle + 2.0 * np.pi * inner[None, :] / rows
    twiddle = np.stack([np.cos(angle), -np.sin(angle), np.cos(odd), -np.sin(odd)], 1)
    twiddle = np.repeat(twiddle.astype(np.float32)[:, :, None, :], 8, 2)
    angle = 2.0 * np.pi * (inner[:, None] * inner[None, :] % half) / half
    cosine, sine = np.cos(angle), np.sin(angle)
    forward = np.block([[cosine, -sine], [sine, cosine]]).astype(np.float32)
    backward = (forward.T / (blocks * rows)).astype(np.float32)

    def split(table):
        high = table.astype(jnp.bfloat16)
        return [high, (table - high.astype(np.float32)).astype(jnp.bfloat16)]

    return twiddle, np.stack(split(forward) + split(backward))


def kernel(
    blocks, chans, zs, signal_in, filt_in, tokens_in, features, weight, twiddle_in, dft_in,
    recv_o, decoded,
    signal, filt, tokens,
    send_x, send_f, send_g, recv_x, recv_f, recv_g, send_o,
    work, wave, spec_x, spec_h, shifted, reversal,
    corr_send, corr_recv, seed_send, seed_recv, rows_held,
    feats, weights, twiddle, dft, query, own, gated,
    part_send, part_recv, part_own, last_send, last_recv,
    local_sem, send_sem, recv_sem,
):
    me, chan = lax.axis_index("pos"), lax.axis_index("chan")
    rows, width = signal.shape
    mine = width // blocks
    slots = blocks + 1
    chunks = mine // GROUP
    per = LANES // mine
    strips = width // LANES
    ys = chans // zs
    z_here, y_here = chan // ys, lax.rem(chan, ys)
    planes = blocks // 4
    stride = 5
    mirror = (3 - me // planes) * planes + lax.rem(me, planes)
    steps = tokens.shape[1]
    samples = tokens.shape[2]
    columns = decoded.shape[1]

    loads = [
        pltpu.make_async_copy(src, dst, local_sem.at[i])
        for i, (src, dst) in enumerate(
            (
                (signal_in, signal),
                (filt_in, filt),
                (tokens_in, tokens.at[0]),
                (dft_in, dft),
                (twiddle_in, twiddle),
                (features, feats),
                (weight, weights),
            )
        )
    ]
    barrier = pltpu.get_barrier_semaphore()

    def greet(i, carry):
        pl.semaphore_signal(
            barrier, inc=1, device_id={"pos": lax.rem(me + i, blocks)}, device_id_type=MESH
        )
        return carry

    lax.fori_loop(1, blocks, greet, 0)
    for i in range(1, ys):
        there = z_here * ys + lax.rem(y_here + i, ys)
        pl.semaphore_signal(barrier, inc=1, device_id={"chan": there}, device_id_type=MESH)
    across = (1 - z_here) * ys + y_here
    pl.semaphore_signal(
        barrier, inc=1, device_id={"pos": mirror, "chan": across}, device_id_type=MESH
    )

    loads[0].start()

    def eye(size):
        return (
            lax.broadcasted_iota(jnp.int32, (size, size), 0)
            == lax.broadcasted_iota(jnp.int32, (size, size), 1)
        ).astype(F32).astype(BF16)

    eye_lanes = eye(LANES)

    def flipped(block):
        turned = lax.dot_general(eye_lanes, block, NT, preferred_element_type=F32)
        return turned.astype(BF16)

    loads[0].wait()
    for load in loads[1:]:
        load.start()
    row_id = lax.broadcasted_iota(jnp.int32, (rows, rows), 0)
    col_id = lax.broadcasted_iota(jnp.int32, (rows, rows), 1)
    for t in range(steps):
        back = (row_id + col_id == t) | (row_id + col_id == t + rows)
        reversal[:, t * rows : (t + 1) * rows] = back.astype(F32).astype(BF16)
    for s in range(strips):
        strip = pl.ds(s * LANES, LANES)
        owners = pl.ds(s * per, per)
        send_x[owners] = flipped(signal[:, strip]).reshape(per, mine, rows)
    pl.semaphore_wait(barrier, (blocks - 1) + (ys - 1) + 1)

    def spread(source, target, slot, start=1, stop=blocks, sent=None):
        def one(i, carry):
            there = lax.rem(me + stride * i, blocks)
            pltpu.make_async_remote_copy(
                src_ref=source(there),
                dst_ref=target,
                send_sem=send_sem.at[slot if sent is None else sent],
                recv_sem=recv_sem.at[slot],
                device_id={"pos": there},
                device_id_type=MESH,
            ).start()
            return carry

        lax.fori_loop(start, stop, one, 0)

    def all_of(source, target, slot, count=blocks - 1):
        others = pl.ds(0, count)
        return pltpu.make_async_remote_copy(
            src_ref=source.at[others],
            dst_ref=target.at[others],
            send_sem=send_sem.at[slot],
            recv_sem=recv_sem.at[slot],
            device_id={"pos": lax.rem(me + 1, blocks)},
            device_id_type=MESH,
        )

    step_ = max(blocks // 4, 1)
    first, second = 1 + step_, 1 + 3 * step_

    def left(source, target, slot, count):
        if count:
            all_of(source, target, slot, count).wait_send()

    def spread_x(start, stop, wave_):
        spread(lambda there: send_x.at[there], recv_x.at[me], 0, start, stop, wave_)

    def spread_f(start, stop, wave_):
        spread(lambda there: send_f.at[there], recv_f.at[me], 1, start, stop, wave_)

    def spread_g(start, stop, wave_):
        spread(lambda there: send_g.at[0, there], recv_g.at[0, me], 3, start, stop, wave_)

    spread_x(1, first, 12)
    spread_x(first, second, 13)
    recv_x[me] = send_x[me]
    loads[1].wait()
    for s in range(strips):
        strip = pl.ds(s * LANES, LANES)
        send_f[pl.ds(s * per, per)] = flipped(filt[0, :, strip]).reshape(per, mine, rows)
    recv_f[me] = send_f[me]

    lane = lax.broadcasted_iota(jnp.int32, (1, LANES), 1)

    @pl.when(me == 0)
    def _():
        x_head = signal[0:16, :].astype(F32)
        g_head = filt[1, 0:16, :].astype(F32)
        for t in range(steps):
            row = x_head[0:1] * g_head[t : t + 1]
            for r in range(1, t + 1):
                row = row + x_head[r : r + 1] * g_head[t - r : t - r + 1]
            for s in range(strips):
                part = row[:, s * LANES : (s + 1) * LANES]
                for i in range(per):
                    shift = (t * mine - i * mine) % LANES
                    moved = pltpu.roll(part, shift, 1) if shift else part
                    inside = (lane >= t * mine) & (lane < (t + 1) * mine)
                    before = corr_send[s * per + i] if t else jnp.zeros((1, LANES), F32)
                    corr_send[s * per + i] = jnp.where(inside, moved, before)
        spread(lambda there: corr_send.at[there], corr_recv, 2)
        corr_recv[...] = corr_send[0]

    for s in range(strips):
        strip = pl.ds(s * LANES, LANES)
        turned = flipped(filt[1, :, strip]).reshape(per, chunks, GROUP, rows)
        for k in range(chunks):
            send_g[k, pl.ds(s * per, per)] = turned[:, k]
    for k in range(chunks):
        recv_g[k, me] = send_g[k, me]

    left(send_x, recv_x, 12, step_)
    spread_x(second, blocks, 14)
    spread_f(1, first, 14)

    loads[2].wait()
    token_copy = pltpu.make_async_remote_copy(
        src_ref=tokens.at[0], dst_ref=tokens.at[1], send_sem=send_sem.at[10], recv_sem=recv_sem.at[10],
        device_id={"pos": mirror}, device_id_type=MESH,
    )
    token_copy.start()
    for load in loads[3:6]:
        load.wait()

    vocab = feats.shape[1]
    same_place = lax.broadcasted_iota(jnp.int32, (samples, samples), 0) == lax.broadcasted_iota(
        jnp.int32, (samples, samples), 1
    )
    for group in range(2):
        if group == 1:
            token_copy.wait_recv()
        for t in range(steps):
            row = tokens[group, t : t + 1, :].astype(F32)
            column = jnp.sum(jnp.where(same_place, row, 0.0), axis=1, keepdims=True).astype(jnp.int32)
            hot = column == lax.broadcasted_iota(jnp.int32, (samples, vocab), 1)
            hot = hot.astype(F32).astype(BF16)
            part = pl.ds((group * steps + t) * samples, samples)
            query[part] = jnp.dot(hot, feats[0], preferred_element_type=F32).astype(BF16)
            own[part] = jnp.dot(hot, feats[1], preferred_element_type=F32) * jnp.dot(
                hot, feats[2], preferred_element_type=F32
            )

    order = frequency_order(blocks)
    half = rows // 2

    def tiles(body):
        def step(i, carry):
            body(pl.ds(pl.multiple_of(i * 8, 8), 8))
            return carry

        lax.fori_loop(0, GROUP // 8, step, 0)

    real, imag = pl.ds(0, half), pl.ds(half, half)

    def forward_tile(same, diff):
        def body(top):
            def put_lower(slot, re, im):
                wave[slot, 0, top, real] = re
                if im is not None:
                    wave[slot, 0, top, imag] = im

            def put_upper(slot, re, im):
                ar = wave[slot, 0, top, real]
                if im is None:
                    ai = im = jnp.zeros_like(re)
                else:
                    ai = wave[slot, 0, top, imag]
                br, bi = spin((re, im), order[slot], 4 * blocks, -1)
                for part, (vr, vi) in enumerate(((ar + br, ai + bi), (ar - br, ai - bi))):
                    c, s = twiddle[slot, 2 * part], twiddle[slot, 2 * part + 1]
                    wave[slot, part, top, real] = vr * c - vi * s
                    wave[slot, part, top, imag] = vr * s + vi * c

            for across, put in ((real, put_lower), (imag, put_upper)):
                outer_forward(
                    blocks,
                    lambda n, across=across: work[same, n, top, across],
                    lambda n, across=across: work[diff, n, top, across],
                    put,
                )

        return body

    def backward_tile(top):
        def take_lower(slot):
            turned = []
            for part in range(2):
                c, s = twiddle[slot, 2 * part], twiddle[slot, 2 * part + 1]
                re, im = wave[slot, part, top, real], wave[slot, part, top, imag]
                turned.append((re * c + im * s, im * c - re * s))
            (er, ei), (vr, vi) = turned
            br, bi = spin((er - vr, ei - vi), order[slot], 4 * blocks, 1)
            wave[slot, 0, top, real] = br
            wave[slot, 0, top, imag] = bi
            return er + vr, ei + vi

        def take_upper(slot):
            return wave[slot, 0, top, real], wave[slot, 0, top, imag]

        for across, take in ((real, take_lower), (imag, take_upper)):

            def put(n, value, across=across):
                work[0, n, top, across] = value

            outer_backward(blocks, take, put)

    group = max(g for g in range(1, 12) if slots % g == 0)

    def split(value):
        high = value.astype(BF16)
        return high, (value - high.astype(F32)).astype(BF16)

    def inner(value, table):
        high, low = split(value)
        dot = functools.partial(jnp.dot, preferred_element_type=F32)
        return dot(high, dft[table]) + dot(low, dft[table]) + dot(high, dft[table + 1])

    def by_slots(body):
        def step(i, carry):
            body(pl.ds(i * group, group))
            return carry

        lax.fori_loop(0, slots // group, step, 0)

    flat = (group * 2 * GROUP, rows)
    deep = (group, 2, GROUP, rows)

    left(send_x, recv_x, 13, 2 * step_)
    spread_f(first, second, 15)
    left(send_x, recv_x, 14, blocks - second + step_)
    spread_f(second, blocks, 16)
    spread_g(1, first + step_, 17)

    all_of(send_x, recv_x, 0).wait_recv()
    bundle = 8 if blocks % 8 == 0 else blocks

    def reverse(i, carry):
        which = pl.ds(i * bundle, bundle)
        taken = recv_x[which].reshape(bundle * mine, rows)
        turned = jnp.dot(taken, reversal[...], preferred_element_type=F32).astype(BF16)
        for t in range(steps):
            part = turned[:, t * rows : (t + 1) * rows]
            shifted[t, which] = part.reshape(bundle, mine, rows)
        return carry

    lax.fori_loop(0, blocks // bundle, reverse, 0)
    for k in range(chunks):
        part = pl.ds(k * GROUP, GROUP)

        def widen(n, carry):
            work[0, n] = recv_x[n, part, :].astype(F32)
            return carry

        lax.fori_loop(0, blocks, widen, 0)
        tiles(forward_tile(0, 0))

        def to_spectrum(which, k=k):
            spec_x[k, which] = inner(wave[which].reshape(flat), 0).reshape(deep)

        by_slots(to_spectrum)

    left(send_f, recv_f, 15, 2 * step_)
    spread_g(first + step_, blocks, 17)
    all_of(send_f, recv_f, 1).wait_recv()
    lanes_here = lax.broadcasted_iota(jnp.int32, (mine, LANES), 1)

    def add_block(n, sums, first):
        near = recv_f[blocks - 1 - n].astype(F32)
        if not first:
            far = recv_f[blocks - n, :, 0:LANES].astype(F32)
        result = []
        for t in range(steps):
            x = shifted[t, n].astype(F32)
            other = jnp.zeros((mine, LANES), F32) if first else far
            total = x[:, 0:LANES] * jnp.where(lanes_here > t, near[:, 0:LANES], other)
            for h in range(1, rows // LANES):
                total = total + x[:, h * LANES : (h + 1) * LANES] * near[:, h * LANES : (h + 1) * LANES]
            result.append(sums[t] + total)
        return tuple(result)

    sums = add_block(0, tuple(jnp.zeros((mine, LANES), F32) for _ in range(steps)), True)
    sums = lax.fori_loop(1, blocks, lambda n, c: add_block(n, c, False), sums)
    channel = lax.broadcasted_iota(jnp.int32, (mine, LANES), 0)
    head = recv_f[0, :, 0:LANES].astype(F32)
    seed_rows = jnp.zeros((mine, LANES), F32)
    head_rows = jnp.zeros((mine, LANES), F32)
    for t in range(steps):
        place = lanes_here == t * mine + channel
        seed_rows += jnp.where(place, jnp.sum(sums[t], axis=1, keepdims=True), 0.0)
        value = jnp.sum(jnp.where(lanes_here == t, head, 0.0), axis=1, keepdims=True)
        head_rows += jnp.where(place, value, 0.0)

    @pl.when(me != 0)
    def _():
        pltpu.make_async_remote_copy(
            src_ref=corr_send.at[0], dst_ref=corr_recv, send_sem=send_sem.at[2],
            recv_sem=recv_sem.at[2], device_id={"pos": 0}, device_id_type=MESH,
        ).wait_recv()

    seed_row = jnp.sum(seed_rows, axis=0, keepdims=True) + corr_recv[...]
    seed_send[:, 0:LANES] = seed_row.astype(BF16).astype(F32)
    seed_send[:, LANES : 2 * LANES] = jnp.sum(head_rows, axis=0, keepdims=True)
    spread(lambda there: seed_send, seed_recv.at[me], 4)
    seed_recv[me] = seed_send[...]
    for k in range(1, chunks):
        spread(lambda there, k=k: send_g.at[k, there], recv_g.at[k, me], 3 + 2 * k)

    def kept_o(k):
        return pltpu.make_async_copy(send_o.at[me, k], recv_o.at[me, k], local_sem.at[k])

    def convolve(k):
        slot = 3 + 2 * k
        all_of(send_g.at[k], recv_g.at[k], slot).wait_recv()
        part = pl.ds(k * GROUP, GROUP)

        def widen(n, carry):
            early, late = recv_f[n, part, :].astype(F32), recv_g[k, n].astype(F32)
            work[0, n] = early + late
            work[1, n] = early - late
            return carry

        lax.fori_loop(0, blocks, widen, 0)
        tiles(forward_tile(0, 1))

        def through(which):
            h = inner(wave[which].reshape(flat), 0)
            x = spec_x[k, which].reshape(flat)
            hr, hi, xr, xi = h[:, :half], h[:, half:], x[:, :half], x[:, half:]
            spec_h[:, real] = hr * xr - hi * xi
            spec_h[:, imag] = hr * xi + hi * xr
            wave[which] = inner(spec_h[...], 2).reshape(deep)

        by_slots(through)
        tiles(backward_tile)

        def narrow(n, carry):
            send_o[n, k] = work[0, n].astype(BF16)
            return carry

        lax.fori_loop(0, blocks, narrow, 0)
        spread(lambda there: send_o.at[there, k], recv_o.at[me, k], 6 + 2 * k)
        kept_o(k).start()

    def decode():
        all_of(seed_recv, seed_recv, 4).wait_recv()
        which = lax.broadcasted_iota(jnp.int32, (blocks, LANES), 1) // mine
        mod = lax.rem(lax.broadcasted_iota(jnp.int32, (blocks, LANES), 0), per)
        pick = (
            lax.broadcasted_iota(jnp.int32, (strips, blocks), 1) // per
            == lax.broadcasted_iota(jnp.int32, (strips, blocks), 0)
        ).astype(F32).astype(BF16)
        for part in range(2):
            taken = seed_recv[:, 0, part * LANES : (part + 1) * LANES]
            for t in range(steps):
                lined = jnp.zeros((blocks, LANES), F32)
                for i in range(per):
                    shift = ((i - t) * mine) % LANES
                    moved = pltpu.roll(taken, shift, 1) if shift else taken
                    lined = jnp.where((which == i) & (mod == i), moved, lined)
                rows_held[part * steps + t] = jnp.dot(
                    pick, lined.astype(BF16), preferred_element_type=F32
                )
        loads[6].wait()

        count = steps * samples
        for group in (1, 0):
            base = group * count
            for s in range(strips):
                strip = pl.ds(s * LANES, LANES)
                for t in range(steps):
                    total = jnp.broadcast_to(rows_held[t, s : s + 1, :], (samples, LANES))
                    for r in range(t + 1):
                        lag = rows_held[steps + t - r, s : s + 1, :]
                        total = total + lag * own[pl.ds(base + r * samples, samples), strip]
                    part = pl.ds(base + t * samples, samples)
                    gated[part, strip] = (query[part, strip].astype(F32) * total).astype(BF16)
            z = z_here if group == 0 else 1 - z_here

            def product(y, z=z, base=base):
                start = pl.multiple_of((z * ys + y) * columns, LANES)
                return jnp.dot(
                    gated[pl.ds(base, count)], weights[:, pl.ds(start, columns)],
                    preferred_element_type=F32,
                )

            def to_y(i, carry, group=group):
                there = lax.rem(y_here + i, ys)
                part_send[group, there] = product(there).astype(BF16)
                pltpu.make_async_remote_copy(
                    src_ref=part_send.at[group, there], dst_ref=part_recv.at[group, y_here],
                    send_sem=send_sem.at[7 + 4 * group], recv_sem=recv_sem.at[7 + 4 * group],
                    device_id={"chan": z_here * ys + there}, device_id_type=MESH,
                ).start()
                return carry

            lax.fori_loop(1, ys, to_y, 0)
            part_own[group] = product(y_here)

    others = pl.ds(0, ys - 1)
    y_all = [
        pltpu.make_async_remote_copy(
            src_ref=part_send.at[group, others], dst_ref=part_recv.at[group, others],
            send_sem=send_sem.at[7 + 4 * group], recv_sem=recv_sem.at[7 + 4 * group],
            device_id={"chan": z_here * ys + lax.rem(y_here + 1, ys)}, device_id_type=MESH,
        )
        for group in range(2)
    ]
    z_copy = pltpu.make_async_remote_copy(
        src_ref=last_send, dst_ref=last_recv, send_sem=send_sem.at[9], recv_sem=recv_sem.at[9],
        device_id={"pos": mirror, "chan": across}, device_id_type=MESH,
    )

    def add_y(group):
        def one(i, carry):
            part_own[group] += part_recv[group, lax.rem(y_here + i, ys)].astype(F32)
            return carry

        y_all[group].wait_recv()
        lax.fori_loop(1, ys, one, 0)

    convolve(0)
    decode()
    for k in range(1, chunks):
        convolve(k)
    add_y(1)
    last_send[...] = part_own[1].astype(BF16)
    z_copy.start()
    add_y(0)
    z_copy.wait_recv()
    result = (part_own[0] + last_recv[...].astype(F32)).astype(BF16)
    decoded[...] = result

    for k in range(chunks):
        all_of(send_o.at[:, k], recv_o.at[:, k], 6 + 2 * k).wait_recv()
    for k in range(chunks):
        kept_o(k).wait()

    left(send_f, recv_f, 16, blocks - second)
    left(send_g.at[0], recv_g.at[0], 17, blocks - 1)

    @pl.when(me == 0)
    def _():
        all_of(corr_send, corr_send, 2).wait_send()

    for k in range(chunks):
        if k > 0:
            all_of(send_g.at[k], recv_g.at[k], 3 + 2 * k).wait_send()
        all_of(send_o.at[:, k], recv_o.at[:, k], 6 + 2 * k).wait_send()
    all_of(seed_recv, seed_recv, 4).wait_send()
    token_copy.wait_send()
    for copy in y_all:
        copy.wait_send()
    z_copy.wait_send()


def finish(samples, contrib_in, decoded_in, contrib, decoded):
    rows, count = contrib_in.shape[1], decoded_in.shape[0]
    steps = count // samples
    here = lax.broadcasted_iota(jnp.int32, (rows, rows), 0)
    there = lax.broadcasted_iota(jnp.int32, (rows, rows), 1)
    same = (here == there).astype(F32).astype(BF16)
    strip = min(rows, contrib_in.shape[0])
    for s in range(contrib_in.shape[0] // strip):
        part = pl.ds(s * strip, strip)
        turned = lax.dot_general(same, contrib_in[part], NT, preferred_element_type=F32)
        contrib[:, part] = turned.astype(BF16)

    if True:
        to = lax.broadcasted_iota(jnp.int32, (count, count), 0)
        of = lax.broadcasted_iota(jnp.int32, (count, count), 1)
        move = of == lax.rem(to, steps) * samples + to // steps
        moved = jnp.dot(
            move.astype(F32).astype(BF16), decoded_in[...], preferred_element_type=F32
        )
        decoded[...] = moved.reshape(decoded.shape).astype(BF16)


def per_device(chans, prompt_signal, long_filter, sample_tokens, token_features, out_weight):
    blocks = lax.axis_size("pos")
    rows, width = prompt_signal.shape
    samples, steps = sample_tokens.shape
    mine = width // blocks
    slots = blocks + 1
    chunks = mine // GROUP
    zs = 2
    ys = chans // zs
    columns = out_weight.shape[1] // chans
    twiddle, dft = tables(blocks, rows)
    group = max(g for g in range(1, 12) if slots % g == 0)
    vmem, dma = pltpu.VMEM, pltpu.SemaphoreType.DMA
    by_vmem = pl.BlockSpec(memory_space=pltpu.VMEM)
    by_hbm = pl.BlockSpec(memory_space=pl.ANY)
    count = steps * samples
    turned, summed = pl.pallas_call(
        functools.partial(kernel, blocks, chans, zs),
        out_shape=(
            jax.ShapeDtypeStruct((blocks, chunks, GROUP, rows), BF16),
            jax.ShapeDtypeStruct((count, columns), BF16),
        ),
        in_specs=[by_hbm] * 7,
        out_specs=(by_hbm, by_vmem),
        scratch_shapes=[
            vmem(prompt_signal.shape, BF16),
            vmem(long_filter.shape, BF16),
            vmem((2, steps, samples), jnp.int32),
            vmem((blocks, mine, rows), BF16),
            vmem((blocks, mine, rows), BF16),
            vmem((chunks, blocks, GROUP, rows), BF16),
            vmem((blocks, mine, rows), BF16),
            vmem((blocks, mine, rows), BF16),
            vmem((chunks, blocks, GROUP, rows), BF16),
            vmem((blocks, chunks, GROUP, rows), BF16),
            vmem((2, blocks, GROUP, rows), F32),
            vmem((slots, 2, GROUP, rows), F32),
            vmem((chunks, slots, 2, GROUP, rows), F32),
            vmem((group * 2 * GROUP, rows), F32),
            vmem((steps, blocks, mine, rows), BF16),
            vmem((rows, steps * rows), BF16),
            vmem((blocks, 1, LANES), F32),
            vmem((1, LANES), F32),
            vmem((1, 2 * LANES), F32),
            vmem((blocks, 1, 2 * LANES), F32),
            vmem((2 * steps, width // LANES, LANES), F32),
            vmem((3, token_features.shape[0], width), BF16),
            vmem(out_weight.shape, BF16),
            vmem(twiddle.shape, F32),
            vmem(dft.shape, BF16),
            vmem((2 * count, width), BF16),
            vmem((2 * count, width), F32),
            vmem((2 * count, width), BF16),
            vmem((2, ys, count, columns), BF16),
            vmem((2, ys, count, columns), BF16),
            vmem((2, count, columns), F32),
            vmem((count, columns), BF16),
            vmem((count, columns), BF16),
            dma((7,)),
            dma((18,)),
            dma((18,)),
        ],
        compiler_params=pltpu.CompilerParams(
            collective_id=0, has_side_effects=True, vmem_limit_bytes=60 * 2**20
        ),
        name="conv_decode",
    )(
        prompt_signal,
        long_filter,
        sample_tokens.T,
        jnp.transpose(token_features, (1, 0, 2)),
        out_weight,
        jnp.asarray(twiddle),
        jnp.asarray(dft),
    )
    return pl.pallas_call(
        functools.partial(finish, samples),
        out_shape=(
            jax.ShapeDtypeStruct((rows, width), BF16),
            jax.ShapeDtypeStruct((samples, steps, columns), BF16),
        ),
        in_specs=[by_vmem, by_vmem],
        out_specs=(by_vmem, by_vmem),
        name="finish",
    )(turned.reshape(width, rows), summed)


def solution(mesh):
    placed = (
        P("pos", "chan"),
        P(None, "pos", "chan"),
        P("pos", None),
        P(None, None, "chan"),
        P("chan", None),
    )
    return jax.shard_map(
        functools.partial(per_device, mesh.shape["chan"]),
        mesh=mesh,
        in_specs=placed,
        out_specs=(P("pos", "chan"), P("pos", None, "chan")),
        check_vma=False,
    )
```

```python
import functools
import math

import jax
import jax.numpy as jnp
import numpy as np
from jax import lax
from jax.experimental import pallas as pl
from jax.experimental.pallas import tpu as pltpu
from jax.sharding import PartitionSpec as P

MESH = pl.DeviceIdType.MESH
LANES = 128
GROUP = 16
F32 = jnp.float32
BF16 = jnp.bfloat16
NT = (((1,), (1,)), ((), ()))


def turn(value, cosine, sine):
    re, im = value
    near = lambda a, b: abs(a - b) < 1e-12
    if near(sine, 0.0):
        return (re, im) if cosine > 0 else (-re, -im)
    if near(cosine, 0.0):
        return (-im, re) if sine > 0 else (im, -re)
    if near(abs(cosine), abs(sine)):
        scale = abs(cosine)
        a, b = math.copysign(1, cosine), math.copysign(1, sine)
        if a > 0:
            return ((re - im if b > 0 else re + im) * scale, (im + re if b > 0 else im - re) * scale)
        return ((re + im if b > 0 else re - im) * -scale, (im - re if b > 0 else im + re) * -scale)
    return (re * cosine - im * sine, re * sine + im * cosine)


def spin(value, index, period, sign):
    angle = 2.0 * math.pi * index / period
    return turn(value, math.cos(angle), sign * math.sin(angle))


def fft(values, sign):
    size = len(values)
    if size == 1:
        return values
    even, odd = fft(values[::2], sign), fft(values[1::2], sign)
    low, high = [], []
    for k in range(size // 2):
        (er, ei), (tr, ti) = even[k], spin(odd[k], k, size, sign)
        low.append((er + tr, ei + ti))
        high.append((er - tr, ei - ti))
    return low + high


def frequency_order(blocks):
    order = [4 * q + 1 for q in range(blocks // 2)]
    size, factor = blocks, 2
    while size >= 4:
        order += [factor * (4 * q + 1) for q in range(size // 4)]
        size, factor = size // 2, factor * 2
    return order + [0, blocks]


def outer_forward(blocks, same, diff, put):
    half = blocks // 2
    held = [spin((diff(n), -diff(n + half)), n, 2 * blocks, -1) for n in range(half)]
    slot = 0
    for re, im in fft(held, -1):
        put(slot, re, im)
        slot += 1
    size = blocks
    real = [(same(n), same(n + half)) for n in range(half)]
    while size >= 4:
        half, quarter = size // 2, size // 4
        lower = [a + b for a, b in real]
        away = [a - b for a, b in real]
        held = [spin((away[n], -away[n + quarter]), n, size, -1) for n in range(quarter)]
        for re, im in fft(held, -1):
            put(slot, re, im)
            slot += 1
        real = [(lower[n], lower[n + quarter]) for n in range(quarter)]
        size = half
    first, second = real[0]
    put(slot, first + second, None)
    put(slot + 1, first - second, None)


def outer_backward(blocks, take, put):
    first, last = take(blocks - 1)[0] * 0.5, take(blocks)[0] * 0.5
    real = [first + last, first - last]
    size, start = 4, blocks - 2
    while size <= blocks:
        quarter = size // 4
        back = fft([take(start + q) for q in range(quarter)], 1)
        back = [spin(value, n, size, 1) for n, value in enumerate(back)]
        wave = [re for re, _ in back] + [-im for _, im in back]
        real = [a + b for a, b in zip(real, wave)] + [a - b for a, b in zip(real, wave)]
        size, start = size * 2, start - size // 2
    half = blocks // 2
    back = fft([take(q) for q in range(half)], 1)
    for n, value in enumerate(back):
        re, im = spin(value, n, 2 * blocks, 1)
        put(n, real[n] - re)
        put(n + half, real[n + half] + im)


def tables(blocks, rows):
    order = np.array(frequency_order(blocks))
    length, half = 2 * blocks * rows, rows // 2
    inner = np.arange(half)
    angle = 2.0 * np.pi * (order[:, None] * inner[None, :] % length) / length
    odd = angle + 2.0 * np.pi * inner[None, :] / rows
    twiddle = np.stack([np.cos(angle), -np.sin(angle), np.cos(odd), -np.sin(odd)], 1)
    twiddle = np.repeat(twiddle.astype(np.float32)[:, :, None, :], 8, 2)
    angle = 2.0 * np.pi * (inner[:, None] * inner[None, :] % half) / half
    cosine, sine = np.cos(angle), np.sin(angle)
    forward = np.block([[cosine, -sine], [sine, cosine]]).astype(np.float32)
    backward = (forward.T / (blocks * rows)).astype(np.float32)

    def split(table):
        high = table.astype(jnp.bfloat16)
        return [high, (table - high.astype(np.float32)).astype(jnp.bfloat16)]

    return twiddle, np.stack(split(forward) + split(backward))


def kernel(
    blocks, chans, zs, signal_in, filt_in, tokens_in, features, weight, twiddle_in, dft_in,
    recv_o, decoded,
    signal, filt, tokens,
    send_x, send_f, send_g, recv_x, recv_f, recv_g, send_o,
    work, wave, spec_x, spec_h, shifted, reversal,
    corr_send, corr_recv, seed_send, seed_recv, rows_held,
    feats, weights, twiddle, dft, query, own, gated,
    part_send, part_recv, part_own, last_send, last_recv,
    local_sem, send_sem, recv_sem,
):
    me, chan = lax.axis_index("pos"), lax.axis_index("chan")
    rows, width = signal.shape
    mine = width // blocks
    slots = blocks + 1
    chunks = mine // GROUP
    per = LANES // mine
    strips = width // LANES
    ys = chans // zs
    z_here, y_here = chan // ys, lax.rem(chan, ys)
    planes = blocks // 4
    stride = 5
    mirror = (3 - me // planes) * planes + lax.rem(me, planes)
    steps = tokens.shape[1]
    samples = tokens.shape[2]
    columns = decoded.shape[1]

    loads = [
        pltpu.make_async_copy(src, dst, local_sem.at[i])
        for i, (src, dst) in enumerate(
            (
                (signal_in, signal),
                (filt_in, filt),
                (tokens_in, tokens.at[0]),
                (dft_in, dft),
                (twiddle_in, twiddle),
                (features, feats),
                (weight, weights),
            )
        )
    ]
    barrier = pltpu.get_barrier_semaphore()

    def greet(i, carry):
        pl.semaphore_signal(
            barrier, inc=1, device_id={"pos": lax.rem(me + i, blocks)}, device_id_type=MESH
        )
        return carry

    lax.fori_loop(1, blocks, greet, 0)
    for i in range(1, ys):
        there = z_here * ys + lax.rem(y_here + i, ys)
        pl.semaphore_signal(barrier, inc=1, device_id={"chan": there}, device_id_type=MESH)
    across = (1 - z_here) * ys + y_here
    pl.semaphore_signal(
        barrier, inc=1, device_id={"pos": mirror, "chan": across}, device_id_type=MESH
    )

    loads[0].start()

    def eye(size):
        return (
            lax.broadcasted_iota(jnp.int32, (size, size), 0)
            == lax.broadcasted_iota(jnp.int32, (size, size), 1)
        ).astype(F32).astype(BF16)

    eye_lanes = eye(LANES)

    def flipped(block):
        turned = lax.dot_general(eye_lanes, block, NT, preferred_element_type=F32)
        return turned.astype(BF16)

    loads[0].wait()
    for load in loads[1:]:
        load.start()
    row_id = lax.broadcasted_iota(jnp.int32, (rows, rows), 0)
    col_id = lax.broadcasted_iota(jnp.int32, (rows, rows), 1)
    for t in range(steps):
        back = (row_id + col_id == t) | (row_id + col_id == t + rows)
        reversal[:, t * rows : (t + 1) * rows] = back.astype(F32).astype(BF16)
    for s in range(strips):
        strip = pl.ds(s * LANES, LANES)
        owners = pl.ds(s * per, per)
        send_x[owners] = flipped(signal[:, strip]).reshape(per, mine, rows)
    pl.semaphore_wait(barrier, (blocks - 1) + (ys - 1) + 1)

    def spread(source, target, slot, start=1, stop=blocks, sent=None):
        def one(i, carry):
            there = lax.rem(me + stride * i, blocks)
            pltpu.make_async_remote_copy(
                src_ref=source(there),
                dst_ref=target,
                send_sem=send_sem.at[slot if sent is None else sent],
                recv_sem=recv_sem.at[slot],
                device_id={"pos": there},
                device_id_type=MESH,
            ).start()
            return carry

        lax.fori_loop(start, stop, one, 0)

    def all_of(source, target, slot, count=blocks - 1):
        others = pl.ds(0, count)
        return pltpu.make_async_remote_copy(
            src_ref=source.at[others],
            dst_ref=target.at[others],
            send_sem=send_sem.at[slot],
            recv_sem=recv_sem.at[slot],
            device_id={"pos": lax.rem(me + 1, blocks)},
            device_id_type=MESH,
        )

    step_ = max(blocks // 4, 1)
    first, second = 1 + step_, 1 + 3 * step_

    def left(source, target, slot, count):
        if count:
            all_of(source, target, slot, count).wait_send()

    def spread_x(start, stop, wave_):
        spread(lambda there: send_x.at[there], recv_x.at[me], 0, start, stop, wave_)

    def spread_f(start, stop, wave_):
        spread(lambda there: send_f.at[there], recv_f.at[me], 1, start, stop, wave_)

    def spread_g(start, stop, wave_):
        spread(lambda there: send_g.at[0, there], recv_g.at[0, me], 3, start, stop, wave_)

    spread_x(1, first, 12)
    spread_x(first, second, 13)
    recv_x[me] = send_x[me]
    loads[1].wait()
    for s in range(strips):
        strip = pl.ds(s * LANES, LANES)
        send_f[pl.ds(s * per, per)] = flipped(filt[0, :, strip]).reshape(per, mine, rows)
    recv_f[me] = send_f[me]

    lane = lax.broadcasted_iota(jnp.int32, (1, LANES), 1)

    @pl.when(me == 0)
    def _():
        x_head = signal[0:16, :].astype(F32)
        g_head = filt[1, 0:16, :].astype(F32)
        for t in range(steps):
            row = x_head[0:1] * g_head[t : t + 1]
            for r in range(1, t + 1):
                row = row + x_head[r : r + 1] * g_head[t - r : t - r + 1]
            for s in range(strips):
                part = row[:, s * LANES : (s + 1) * LANES]
                for i in range(per):
                    shift = (t * mine - i * mine) % LANES
                    moved = pltpu.roll(part, shift, 1) if shift else part
                    inside = (lane >= t * mine) & (lane < (t + 1) * mine)
                    before = corr_send[s * per + i] if t else jnp.zeros((1, LANES), F32)
                    corr_send[s * per + i] = jnp.where(inside, moved, before)
        spread(lambda there: corr_send.at[there], corr_recv, 2)
        corr_recv[...] = corr_send[0]

    for s in range(strips):
        strip = pl.ds(s * LANES, LANES)
        turned = flipped(filt[1, :, strip]).reshape(per, chunks, GROUP, rows)
        for k in range(chunks):
            send_g[k, pl.ds(s * per, per)] = turned[:, k]
    for k in range(chunks):
        recv_g[k, me] = send_g[k, me]

    left(send_x, recv_x, 12, step_)
    spread_x(second, blocks, 14)
    spread_f(1, first, 14)

    loads[2].wait()
    token_copy = pltpu.make_async_remote_copy(
        src_ref=tokens.at[0], dst_ref=tokens.at[1], send_sem=send_sem.at[10], recv_sem=recv_sem.at[10],
        device_id={"pos": mirror}, device_id_type=MESH,
    )
    token_copy.start()
    for load in loads[3:6]:
        load.wait()

    vocab = feats.shape[1]
    same_place = lax.broadcasted_iota(jnp.int32, (samples, samples), 0) == lax.broadcasted_iota(
        jnp.int32, (samples, samples), 1
    )
    for group in range(2):
        if group == 1:
            token_copy.wait_recv()
        for t in range(steps):
            row = tokens[group, t : t + 1, :].astype(F32)
            column = jnp.sum(jnp.where(same_place, row, 0.0), axis=1, keepdims=True).astype(jnp.int32)
            hot = column == lax.broadcasted_iota(jnp.int32, (samples, vocab), 1)
            hot = hot.astype(F32).astype(BF16)
            part = pl.ds((group * steps + t) * samples, samples)
            query[part] = jnp.dot(hot, feats[0], preferred_element_type=F32).astype(BF16)
            own[part] = jnp.dot(hot, feats[1], preferred_element_type=F32) * jnp.dot(
                hot, feats[2], preferred_element_type=F32
            )

    order = frequency_order(blocks)
    half = rows // 2

    def tiles(body):
        def step(i, carry):
            body(pl.ds(pl.multiple_of(i * 8, 8), 8))
            return carry

        lax.fori_loop(0, GROUP // 8, step, 0)

    real, imag = pl.ds(0, half), pl.ds(half, half)

    def forward_tile(same, diff):
        def body(top):
            def put_lower(slot, re, im):
                wave[slot, 0, top, real] = re
                if im is not None:
                    wave[slot, 0, top, imag] = im

            def put_upper(slot, re, im):
                ar = wave[slot, 0, top, real]
                if im is None:
                    ai = im = jnp.zeros_like(re)
                else:
                    ai = wave[slot, 0, top, imag]
                br, bi = spin((re, im), order[slot], 4 * blocks, -1)
                for part, (vr, vi) in enumerate(((ar + br, ai + bi), (ar - br, ai - bi))):
                    c, s = twiddle[slot, 2 * part], twiddle[slot, 2 * part + 1]
                    wave[slot, part, top, real] = vr * c - vi * s
                    wave[slot, part, top, imag] = vr * s + vi * c

            for across, put in ((real, put_lower), (imag, put_upper)):
                outer_forward(
                    blocks,
                    lambda n, across=across: work[same, n, top, across],
                    lambda n, across=across: work[diff, n, top, across],
                    put,
                )

        return body

    def backward_tile(top):
        def take_lower(slot):
            turned = []
            for part in range(2):
                c, s = twiddle[slot, 2 * part], twiddle[slot, 2 * part + 1]
                re, im = wave[slot, part, top, real], wave[slot, part, top, imag]
                turned.append((re * c + im * s, im * c - re * s))
            (er, ei), (vr, vi) = turned
            br, bi = spin((er - vr, ei - vi), order[slot], 4 * blocks, 1)
            wave[slot, 0, top, real] = br
            wave[slot, 0, top, imag] = bi
            return er + vr, ei + vi

        def take_upper(slot):
            return wave[slot, 0, top, real], wave[slot, 0, top, imag]

        for across, take in ((real, take_lower), (imag, take_upper)):

            def put(n, value, across=across):
                work[0, n, top, across] = value

            outer_backward(blocks, take, put)

    group = max(g for g in range(1, 40) if slots % g == 0)

    def split(value):
        high = value.astype(BF16)
        return high, (value - high.astype(F32)).astype(BF16)

    def inner(value, table):
        high, low = split(value)
        dot = functools.partial(jnp.dot, preferred_element_type=F32)
        both = dot(jnp.concatenate([high, low], 0), dft[table])
        count = value.shape[0]
        return both[:count] + both[count:] + dot(high, dft[table + 1])

    def by_slots(body):
        def step(i, carry):
            body(pl.ds(i * group, group))
            return carry

        lax.fori_loop(0, slots // group, step, 0)

    flat = (group * 2 * GROUP, rows)
    deep = (group, 2, GROUP, rows)

    left(send_x, recv_x, 13, 2 * step_)
    spread_f(first, second, 15)
    left(send_x, recv_x, 14, blocks - second + step_)
    spread_f(second, blocks, 16)
    spread_g(1, first + step_, 17)

    all_of(send_x, recv_x, 0).wait_recv()
    bundle = 8 if blocks % 8 == 0 else blocks

    def reverse(i, carry):
        which = pl.ds(i * bundle, bundle)
        taken = recv_x[which].reshape(bundle * mine, rows)
        turned = jnp.dot(taken, reversal[...], preferred_element_type=F32).astype(BF16)
        for t in range(steps):
            part = turned[:, t * rows : (t + 1) * rows]
            shifted[t, which] = part.reshape(bundle, mine, rows)
        return carry

    lax.fori_loop(0, blocks // bundle, reverse, 0)
    for k in range(chunks):
        part = pl.ds(k * GROUP, GROUP)

        def widen(n, carry):
            work[0, n] = recv_x[n, part, :].astype(F32)
            return carry

        lax.fori_loop(0, blocks, widen, 0)
        tiles(forward_tile(0, 0))

        def to_spectrum(which, k=k):
            spec_x[k, which] = inner(wave[which].reshape(flat), 0).reshape(deep)

        by_slots(to_spectrum)

    left(send_f, recv_f, 15, 2 * step_)
    spread_g(first + step_, blocks, 17)
    all_of(send_f, recv_f, 1).wait_recv()
    lanes_here = lax.broadcasted_iota(jnp.int32, (mine, LANES), 1)

    def add_block(n, sums, first):
        near = recv_f[blocks - 1 - n].astype(F32)
        if not first:
            far = recv_f[blocks - n, :, 0:LANES].astype(F32)
        result = []
        for t in range(steps):
            x = shifted[t, n].astype(F32)
            other = jnp.zeros((mine, LANES), F32) if first else far
            total = x[:, 0:LANES] * jnp.where(lanes_here > t, near[:, 0:LANES], other)
            for h in range(1, rows // LANES):
                total = total + x[:, h * LANES : (h + 1) * LANES] * near[:, h * LANES : (h + 1) * LANES]
            result.append(sums[t] + total)
        return tuple(result)

    sums = add_block(0, tuple(jnp.zeros((mine, LANES), F32) for _ in range(steps)), True)
    sums = lax.fori_loop(1, blocks, lambda n, c: add_block(n, c, False), sums)
    channel = lax.broadcasted_iota(jnp.int32, (mine, LANES), 0)
    head = recv_f[0, :, 0:LANES].astype(F32)
    seed_rows = jnp.zeros((mine, LANES), F32)
    head_rows = jnp.zeros((mine, LANES), F32)
    for t in range(steps):
        place = lanes_here == t * mine + channel
        seed_rows += jnp.where(place, jnp.sum(sums[t], axis=1, keepdims=True), 0.0)
        value = jnp.sum(jnp.where(lanes_here == t, head, 0.0), axis=1, keepdims=True)
        head_rows += jnp.where(place, value, 0.0)

    @pl.when(me != 0)
    def _():
        pltpu.make_async_remote_copy(
            src_ref=corr_send.at[0], dst_ref=corr_recv, send_sem=send_sem.at[2],
            recv_sem=recv_sem.at[2], device_id={"pos": 0}, device_id_type=MESH,
        ).wait_recv()

    seed_row = jnp.sum(seed_rows, axis=0, keepdims=True) + corr_recv[...]
    seed_send[:, 0:LANES] = seed_row.astype(BF16).astype(F32)
    seed_send[:, LANES : 2 * LANES] = jnp.sum(head_rows, axis=0, keepdims=True)
    spread(lambda there: seed_send, seed_recv.at[me], 4)
    seed_recv[me] = seed_send[...]
    for k in range(1, chunks):
        spread(lambda there, k=k: send_g.at[k, there], recv_g.at[k, me], 3 + 2 * k)

    def kept_o(k):
        return pltpu.make_async_copy(send_o.at[me, k], recv_o.at[me, k], local_sem.at[k])

    def convolve(k):
        slot = 3 + 2 * k
        all_of(send_g.at[k], recv_g.at[k], slot).wait_recv()
        part = pl.ds(k * GROUP, GROUP)

        def widen(n, carry):
            early, late = recv_f[n, part, :].astype(F32), recv_g[k, n].astype(F32)
            work[0, n] = early + late
            work[1, n] = early - late
            return carry

        lax.fori_loop(0, blocks, widen, 0)
        tiles(forward_tile(0, 1))

        def through(which):
            h = inner(wave[which].reshape(flat), 0)
            x = spec_x[k, which].reshape(flat)
            hr, hi, xr, xi = h[:, :half], h[:, half:], x[:, :half], x[:, half:]
            spec_h[:, real] = hr * xr - hi * xi
            spec_h[:, imag] = hr * xi + hi * xr
            wave[which] = inner(spec_h[...], 2).reshape(deep)

        by_slots(through)
        tiles(backward_tile)

        def narrow(n, carry):
            send_o[n, k] = work[0, n].astype(BF16)
            return carry

        lax.fori_loop(0, blocks, narrow, 0)
        spread(lambda there: send_o.at[there, k], recv_o.at[me, k], 6 + 2 * k)
        kept_o(k).start()

    def decode():
        all_of(seed_recv, seed_recv, 4).wait_recv()
        which = lax.broadcasted_iota(jnp.int32, (blocks, LANES), 1) // mine
        mod = lax.rem(lax.broadcasted_iota(jnp.int32, (blocks, LANES), 0), per)
        pick = (
            lax.broadcasted_iota(jnp.int32, (strips, blocks), 1) // per
            == lax.broadcasted_iota(jnp.int32, (strips, blocks), 0)
        ).astype(F32).astype(BF16)
        for part in range(2):
            taken = seed_recv[:, 0, part * LANES : (part + 1) * LANES]
            for t in range(steps):
                lined = jnp.zeros((blocks, LANES), F32)
                for i in range(per):
                    shift = ((i - t) * mine) % LANES
                    moved = pltpu.roll(taken, shift, 1) if shift else taken
                    lined = jnp.where((which == i) & (mod == i), moved, lined)
                rows_held[part * steps + t] = jnp.dot(
                    pick, lined.astype(BF16), preferred_element_type=F32
                )
        loads[6].wait()

        count = steps * samples
        for group in (1, 0):
            base = group * count
            for s in range(strips):
                strip = pl.ds(s * LANES, LANES)
                for t in range(steps):
                    total = jnp.broadcast_to(rows_held[t, s : s + 1, :], (samples, LANES))
                    for r in range(t + 1):
                        lag = rows_held[steps + t - r, s : s + 1, :]
                        total = total + lag * own[pl.ds(base + r * samples, samples), strip]
                    part = pl.ds(base + t * samples, samples)
                    gated[part, strip] = (query[part, strip].astype(F32) * total).astype(BF16)
            z = z_here if group == 0 else 1 - z_here

            def product(y, z=z, base=base):
                start = pl.multiple_of((z * ys + y) * columns, LANES)
                return jnp.dot(
                    gated[pl.ds(base, count)], weights[:, pl.ds(start, columns)],
                    preferred_element_type=F32,
                )

            def to_y(i, carry, group=group):
                there = lax.rem(y_here + i, ys)
                part_send[group, there] = product(there).astype(BF16)
                pltpu.make_async_remote_copy(
                    src_ref=part_send.at[group, there], dst_ref=part_recv.at[group, y_here],
                    send_sem=send_sem.at[7 + 4 * group], recv_sem=recv_sem.at[7 + 4 * group],
                    device_id={"chan": z_here * ys + there}, device_id_type=MESH,
                ).start()
                return carry

            lax.fori_loop(1, ys, to_y, 0)
            part_own[group] = product(y_here)

    others = pl.ds(0, ys - 1)
    y_all = [
        pltpu.make_async_remote_copy(
            src_ref=part_send.at[group, others], dst_ref=part_recv.at[group, others],
            send_sem=send_sem.at[7 + 4 * group], recv_sem=recv_sem.at[7 + 4 * group],
            device_id={"chan": z_here * ys + lax.rem(y_here + 1, ys)}, device_id_type=MESH,
        )
        for group in range(2)
    ]
    z_copy = pltpu.make_async_remote_copy(
        src_ref=last_send, dst_ref=last_recv, send_sem=send_sem.at[9], recv_sem=recv_sem.at[9],
        device_id={"pos": mirror, "chan": across}, device_id_type=MESH,
    )

    def add_y(group):
        def one(i, carry):
            part_own[group] += part_recv[group, lax.rem(y_here + i, ys)].astype(F32)
            return carry

        y_all[group].wait_recv()
        lax.fori_loop(1, ys, one, 0)

    convolve(0)
    decode()
    for k in range(1, chunks):
        convolve(k)
    add_y(1)
    last_send[...] = part_own[1].astype(BF16)
    z_copy.start()
    add_y(0)
    z_copy.wait_recv()
    result = (part_own[0] + last_recv[...].astype(F32)).astype(BF16)
    decoded[...] = result

    for k in range(chunks):
        all_of(send_o.at[:, k], recv_o.at[:, k], 6 + 2 * k).wait_recv()
    for k in range(chunks):
        kept_o(k).wait()

    left(send_f, recv_f, 16, blocks - second)
    left(send_g.at[0], recv_g.at[0], 17, blocks - 1)

    @pl.when(me == 0)
    def _():
        all_of(corr_send, corr_send, 2).wait_send()

    for k in range(chunks):
        if k > 0:
            all_of(send_g.at[k], recv_g.at[k], 3 + 2 * k).wait_send()
        all_of(send_o.at[:, k], recv_o.at[:, k], 6 + 2 * k).wait_send()
    all_of(seed_recv, seed_recv, 4).wait_send()
    token_copy.wait_send()
    for copy in y_all:
        copy.wait_send()
    z_copy.wait_send()


def finish(samples, contrib_in, decoded_in, contrib, decoded):
    rows, count = contrib_in.shape[1], decoded_in.shape[0]
    steps = count // samples
    here = lax.broadcasted_iota(jnp.int32, (rows, rows), 0)
    there = lax.broadcasted_iota(jnp.int32, (rows, rows), 1)
    same = (here == there).astype(F32).astype(BF16)
    strip = min(rows, contrib_in.shape[0])
    for s in range(contrib_in.shape[0] // strip):
        part = pl.ds(s * strip, strip)
        turned = lax.dot_general(same, contrib_in[part], NT, preferred_element_type=F32)
        contrib[:, part] = turned.astype(BF16)

    if True:
        to = lax.broadcasted_iota(jnp.int32, (count, count), 0)
        of = lax.broadcasted_iota(jnp.int32, (count, count), 1)
        move = of == lax.rem(to, steps) * samples + to // steps
        moved = jnp.dot(
            move.astype(F32).astype(BF16), decoded_in[...], preferred_element_type=F32
        )
        decoded[...] = moved.reshape(decoded.shape).astype(BF16)


def per_device(chans, prompt_signal, long_filter, sample_tokens, token_features, out_weight):
    blocks = lax.axis_size("pos")
    rows, width = prompt_signal.shape
    samples, steps = sample_tokens.shape
    mine = width // blocks
    slots = blocks + 1
    chunks = mine // GROUP
    zs = 2
    ys = chans // zs
    columns = out_weight.shape[1] // chans
    twiddle, dft = tables(blocks, rows)
    group = max(g for g in range(1, 40) if slots % g == 0)
    vmem, dma = pltpu.VMEM, pltpu.SemaphoreType.DMA
    by_vmem = pl.BlockSpec(memory_space=pltpu.VMEM)
    by_hbm = pl.BlockSpec(memory_space=pl.ANY)
    count = steps * samples
    turned, summed = pl.pallas_call(
        functools.partial(kernel, blocks, chans, zs),
        out_shape=(
            jax.ShapeDtypeStruct((blocks, chunks, GROUP, rows), BF16),
            jax.ShapeDtypeStruct((count, columns), BF16),
        ),
        in_specs=[by_hbm] * 7,
        out_specs=(by_hbm, by_vmem),
        scratch_shapes=[
            vmem(prompt_signal.shape, BF16),
            vmem(long_filter.shape, BF16),
            vmem((2, steps, samples), jnp.int32),
            vmem((blocks, mine, rows), BF16),
            vmem((blocks, mine, rows), BF16),
            vmem((chunks, blocks, GROUP, rows), BF16),
            vmem((blocks, mine, rows), BF16),
            vmem((blocks, mine, rows), BF16),
            vmem((chunks, blocks, GROUP, rows), BF16),
            vmem((blocks, chunks, GROUP, rows), BF16),
            vmem((2, blocks, GROUP, rows), F32),
            vmem((slots, 2, GROUP, rows), F32),
            vmem((chunks, slots, 2, GROUP, rows), F32),
            vmem((group * 2 * GROUP, rows), F32),
            vmem((steps, blocks, mine, rows), BF16),
            vmem((rows, steps * rows), BF16),
            vmem((blocks, 1, LANES), F32),
            vmem((1, LANES), F32),
            vmem((1, 2 * LANES), F32),
            vmem((blocks, 1, 2 * LANES), F32),
            vmem((2 * steps, width // LANES, LANES), F32),
            vmem((3, token_features.shape[0], width), BF16),
            vmem(out_weight.shape, BF16),
            vmem(twiddle.shape, F32),
            vmem(dft.shape, BF16),
            vmem((2 * count, width), BF16),
            vmem((2 * count, width), F32),
            vmem((2 * count, width), BF16),
            vmem((2, ys, count, columns), BF16),
            vmem((2, ys, count, columns), BF16),
            vmem((2, count, columns), F32),
            vmem((count, columns), BF16),
            vmem((count, columns), BF16),
            dma((7,)),
            dma((18,)),
            dma((18,)),
        ],
        compiler_params=pltpu.CompilerParams(
            collective_id=0, has_side_effects=True, vmem_limit_bytes=60 * 2**20
        ),
        name="conv_decode",
    )(
        prompt_signal,
        long_filter,
        sample_tokens.T,
        jnp.transpose(token_features, (1, 0, 2)),
        out_weight,
        jnp.asarray(twiddle),
        jnp.asarray(dft),
    )
    return pl.pallas_call(
        functools.partial(finish, samples),
        out_shape=(
            jax.ShapeDtypeStruct((rows, width), BF16),
            jax.ShapeDtypeStruct((samples, steps, columns), BF16),
        ),
        in_specs=[by_vmem, by_vmem],
        out_specs=(by_vmem, by_vmem),
        name="finish",
    )(turned.reshape(width, rows), summed)


def solution(mesh):
    placed = (
        P("pos", "chan"),
        P(None, "pos", "chan"),
        P("pos", None),
        P(None, None, "chan"),
        P("chan", None),
    )
    return jax.shard_map(
        functools.partial(per_device, mesh.shape["chan"]),
        mesh=mesh,
        in_specs=placed,
        out_specs=(P("pos", "chan"), P("pos", None, "chan")),
        check_vma=False,
    )
```
